128 devices in a mesh: row: 8 (over z, x_hi), col: 16 (over y, x_lo, core).
Axes of the slice: x: 4 (x_hi: 2, x_lo: 2; x = x_hi * 2 + x_lo), y: 4, z: 4, core: 2. Of those that a mesh axis runs over, the one named last changes fastest.
Arguments:
- fine_in: bfloat16 [256, 2048, 128], P('row', 'col'), may hold values from -6 to 6
- coarse: bfloat16 [64, 32, 128], P('row'), may hold values from -6 to 6
- block_map: int32 [8, 16, 4], P('row', 'col'), may hold values from 0 to 63, as said below
- interp: bfloat16 [4, 128, 256, 2048], P(None, None, 'row', 'col'), may hold values from -0.25 to 0.25
- lift_weight: bfloat16 [32, 128], replicated, may hold values from -1 to 1
- conv_first: bfloat16 [3, 3, 128, 128], replicated, may hold values from -0.1875 to 0.1875
- conv_second: bfloat16 [3, 3, 128, 128], replicated, may hold values from -0.1875 to 0.1875
- cotangent: bfloat16 [256, 2048, 128], P('row', 'col'), may hold values from -6 to 6
Outputs:
- output: bfloat16 [256, 2048, 128], P('row', 'col')
- grad_fine: bfloat16 [256, 2048, 128], P('row', 'col')
- grad_coarse: float32 [64, 32, 128], P('row')
- grad_first: float32 [3, 3, 128, 128], replicated
- grad_second: float32 [3, 3, 128, 128], replicated
- grad_lift: float32 [32, 128], replicated
The draws below stay inside these ranges and needn't reach their ends.
Inputs may be any that keep to these rules, and one draw needn't show every extreme that they name: `block_map`: every block named by tile (i, j) lies in rows i - 1, i or i + 1 of the blocks' rows of 8: from (i - 1) * 8 up to (i + 2) * 8 - 1, within the grid of blocks; each tile with i > 0 names at least one block of row i - 1 (it may name several) and each with i + 1 < 8 at least one of row i + 1.
All inputs are finite; a program needn't handle non-finite values.
Results may differ from the reference program's by a relative error of at most 0.009.
Values may be sent and summed in bfloat16 or wider, within the bound.
A program may use at most 128 MiB of HBM per device.

```python
import jax
import jax.numpy as jnp
from jax import lax

C = 128
CC = 32
BLK = 128
K = 4
FH = 32
FW = 128
CBLK = 8
NH = 256
NW = 2048
NBLK = 64
GNORM = 1024
N_ROW = 8
N_COL = 16


def draw_block_map(key, part):
    key = jax.random.fold_in(key, 7)
    rows_ids = jnp.arange(N_ROW, dtype=jnp.int32)[:, None, None]
    side = jnp.arange(K, dtype=jnp.int32) % 3 - 1
    owner = jnp.clip(rows_ids + side[None, None, :], 0, N_ROW - 1)
    within = jax.random.randint(key, (N_ROW, N_COL, K), 0, CBLK, dtype=jnp.int32)
    within = within.at[:, 0, 0].set(0)
    within = within.at[:, 0, 2].set(CBLK - 1)
    return (owner * CBLK + within).astype(jnp.int32)


def block_levels(stream_key, shape, cuts, least, largest):
    def one(axis_at, parts):
        steps = jax.random.uniform(jax.random.fold_in(jax.random.fold_in(stream_key, 6), axis_at), (parts,), jnp.float32, least / len(cuts), largest / len(cuts))
        return jnp.repeat(jnp.exp(steps), shape[axis_at] // parts).reshape((-1,) + (1,) * (len(shape) - axis_at - 1))

    gain = one(*cuts[0])
    for cut in cuts[1:]:
        gain = gain * one(*cut)
    return gain


def centred(rng, shape, spread, most, pieces=(), kind=jnp.bfloat16):
    values = jax.random.normal(rng, shape, jnp.float32) * spread
    if len(pieces) > 0:
        values = block_levels(rng, shape, pieces, -0.22, 0.18) * values
    return jnp.clip(values, min=-most, max=most).astype(kind)


def setup_inputs(seed: int = 0) -> dict:
    streams_of = jax.random.split(jax.random.key(seed), 9)
    fine_in = centred(streams_of[0], (NH, NW, C), 1.0, 6.0, ((0, 8), (1, 16)))
    coarse = centred(streams_of[1], (NBLK, CC, BLK), 1.0, 6.0, ((0, 8),))
    block_map = draw_block_map(jax.random.fold_in(streams_of[8], 71), 0)
    interp = centred(streams_of[3], (K, BLK, NH, NW), (K * BLK) ** -0.5, 0.25, ((2, 8), (3, 16)))
    lift_weight = centred(streams_of[4], (CC, C), CC ** -0.5, 1.0)
    conv_first = centred(streams_of[5], (3, 3, C, C), (9 * C) ** -0.5, 0.1875)
    conv_second = centred(streams_of[6], (3, 3, C, C), (9 * C) ** -0.5, 0.1875)
    cotangent = centred(streams_of[7], (NH, NW, C), 1.0, 6.0, ((0, 8), (1, 16)))
    return {"fine_in": fine_in, "coarse": coarse, "block_map": block_map, "interp": interp, "lift_weight": lift_weight, "conv_first": conv_first, "conv_second": conv_second, "cotangent": cotangent}


def conv_taps(padded, kernel, rows, cols):
    total = jnp.zeros((rows * cols, kernel.shape[3]), jnp.float32)
    for shift_row in range(3):
        for shift_col in range(3):
            piece = padded[shift_row:shift_row + rows, shift_col:shift_col + cols].reshape(rows * cols, -1)
            total = total + jnp.dot(piece, kernel[shift_row, shift_col], preferred_element_type=jnp.float32)
    return total

def kernel_grad(padded, grad_flat, rows, cols):
    taps_list = []
    for shift_row in range(3):
        for shift_col in range(3):
            piece = padded[shift_row:shift_row + rows, shift_col:shift_col + cols].reshape(rows * cols, -1)
            taps_list.append(lax.dot_general(piece, grad_flat, (((0,), (0,)), ((), ())), preferred_element_type=jnp.float32))
    return jnp.stack(taps_list).reshape(3, 3, taps_list[0].shape[0], taps_list[0].shape[1])

def flipped(kernel):
    return jnp.transpose(jnp.flip(kernel, (0, 1)), (0, 1, 3, 2))

def padding(field):
    return jnp.pad(field, ((1, 1), (1, 1), (0, 0)))

def reference(fine_in, coarse, block_map, interp, lift_weight, conv_first, conv_second, cotangent):
    cells = NH * NW
    chosen = coarse[block_map.reshape(-1)].reshape(N_ROW, N_COL, K, CC, BLK)

    def row_up(index):
        picked = lax.dynamic_index_in_dim(chosen, index, 0, keepdims=False).astype(jnp.float32)
        weights = lax.dynamic_slice_in_dim(interp, index * FH, FH, 2).reshape(K, BLK, FH, N_COL, FW).astype(jnp.float32)
        return jnp.einsum('jkcb,kbyjx->cyjx', picked, weights)
    upsum = lax.map(row_up, jnp.arange(N_ROW, dtype=jnp.int32))
    upward = jnp.transpose(upsum, (1, 0, 2, 3, 4)).reshape(CC, cells).astype(jnp.bfloat16)
    lifted = lax.dot_general(upward, lift_weight, (((0,), (0,)), ((), ())), preferred_element_type=jnp.float32)
    stem = (fine_in.reshape(cells, C).astype(jnp.float32) + lifted).astype(jnp.bfloat16)
    stem_pad = padding(stem.reshape(NH, NW, C))
    first_pre = conv_taps(stem_pad, conv_first, NH, NW)
    first_act = jax.nn.silu(first_pre).astype(jnp.bfloat16)
    act_pad = padding(first_act.reshape(NH, NW, C))
    output = (stem.astype(jnp.float32) + conv_taps(act_pad, conv_second, NH, NW)).astype(jnp.bfloat16)
    cot_flat = cotangent.reshape(cells, C)
    grad_act = conv_taps(padding(cotangent), flipped(conv_second), NH, NW)
    sigma = jax.nn.sigmoid(first_pre)
    grad_pre = (grad_act * (sigma * (1.0 + first_pre * (1.0 - sigma)))).astype(jnp.bfloat16)
    grad_second = kernel_grad(act_pad, cot_flat, NH, NW) / GNORM
    grad_first = kernel_grad(stem_pad, grad_pre, NH, NW) / GNORM
    pre_pad = padding(grad_pre.reshape(NH, NW, C))
    grad_fine = (cot_flat.astype(jnp.float32) + conv_taps(pre_pad, flipped(conv_first), NH, NW)).astype(jnp.bfloat16)
    grad_lift = jnp.dot(upward, grad_fine, preferred_element_type=jnp.float32) / GNORM
    grad_up = lax.dot_general(lift_weight, grad_fine, (((1,), (1,)), ((), ())), preferred_element_type=jnp.float32).astype(jnp.bfloat16)
    grad_grid = grad_up.reshape(CC, N_ROW, FH, N_COL, FW)

    def row_back(index):
        part_grad = lax.dynamic_index_in_dim(grad_grid, index, 1, keepdims=False).astype(jnp.float32)
        weights = lax.dynamic_slice_in_dim(interp, index * FH, FH, 2).reshape(K, BLK, FH, N_COL, FW).astype(jnp.float32)
        return jnp.einsum('cyjx,kbyjx->jkcb', part_grad, weights)
    block_terms = lax.map(row_back, jnp.arange(N_ROW, dtype=jnp.int32)).reshape(N_ROW * N_COL * K, CC, BLK)
    grad_coarse = jax.ops.segment_sum(block_terms, block_map.reshape(-1).astype(jnp.int32), num_segments=NBLK)
    return (output.reshape(NH, NW, C), grad_fine.reshape(NH, NW, C), grad_coarse, grad_first, grad_second, grad_lift)
```

```python
import functools

import jax
import jax.numpy as jnp
from jax import lax
from jax.experimental import pallas as pl
from jax.experimental.pallas import tpu as pltpu
from jax.sharding import PartitionSpec as P

MESH = pl.DeviceIdType.MESH
BF = jnp.bfloat16
F32 = jnp.float32
PITCH = 144
CHUNK = 80


def rows_of(row, count=1, pitch=128):
    start = row * pitch
    if not isinstance(start, int):
        start = pl.multiple_of(start, pitch if pitch == 128 else 16)
    return pl.ds(start, count * pitch)


def pair_conv(x3, wp, first, pairs):
    parts = []
    for j in range(4):
        parts.append(
            jnp.concatenate([x3[rows_of(first + 2 * p + j), :] for p in range(pairs)], 0)
        )
    return jnp.dot(jnp.concatenate(parts, 1), wp[...], preferred_element_type=F32)


def side_conv(pad, wp):
    sides = []
    for base in (6, 135):
        sides.append(
            jnp.concatenate(
                [
                    pad[pl.ds(a * PITCH + base + e, 40, stride=PITCH), :].astype(BF)
                    for a in range(3)
                    for e in range(3)
                ],
                1,
            )
        )
    return jnp.dot(
        jnp.concatenate(sides, 0), wp[0:1152, 0:128], preferred_element_type=F32
    )


def shifted_row(pad, x3, row):
    start = row * PITCH + 8
    for e in range(3):
        x3[rows_of(row), e * 128 : (e + 1) * 128] = pad[pl.ds(start + e - 1, 128), :].astype(BF)


def gate(pre, grad):
    s = 0.5 * (1.0 + jnp.tanh(0.5 * pre))
    return pre * s, grad * (s * (1.0 + pre * (1.0 - s)))


def kernel(
    n_row,
    n_col,
    fine,
    coarse,
    ids,
    interp,
    lift,
    first,
    second,
    cot,
    out,
    grad_fine,
    grad_coarse,
    grad_first,
    grad_second,
    grad_lift,
    fine_v,
    interp_v,
    weights_it,
    window,
    lift_v,
    first_v,
    second_v,
    wp_first,
    wp_second,
    wp_first_f,
    wp_second_f,
    pad_cot,
    pad_stem,
    pad_act,
    pad_pre,
    x3_cot,
    x3_stem,
    x3_act,
    x3_pre,
    cot_z,
    pre_z,
    stem_v,
    grad_act,
    gf_v,
    out_v,
    mix,
    edge_send,
    land_row,
    land_col,
    land_corner,
    taps,
    local,
    land0,
    half,
    land1,
    land2,
    final,
    wide,
    coarse_wide,
    lift_wide,
    copy_sem,
    out_sem,
    coarse_send,
    coarse_recv,
    halo_send,
    halo_recv,
    s0_send,
    s0_recv,
    s1_send,
    s1_recv,
    s2_send,
    s2_recv,
    s3_send,
    s3_recv,
    s4_send,
    s4_recv,
):
    r = lax.axis_index("row")
    c = lax.axis_index("col")
    nq = n_col // 2
    q = lax.div(c, 2)
    h = lax.rem(c, 2)
    sibling = c + 1 - 2 * h
    own = h * nq + q
    up = lax.rem(r + n_row - 1, n_row)
    down = lax.rem(r + 1, n_row)
    left = lax.rem(c + n_col - 1, n_col)
    right = lax.rem(c + 1, n_col)
    q_peers = [lax.rem(q + d, nq) for d in range(1, nq)]
    r_peers = [lax.rem(r + d, n_row) for d in range(1, n_row)]

    around = [
        (up, c), (down, c), (r, left), (r, right),
        (up, left), (up, right), (down, left), (down, right),
    ]
    barrier = pltpu.get_barrier_semaphore()
    peers = (
        around
        + [(r, 2 * peer + h) for peer in q_peers]
        + [(peer, c) for peer in r_peers[1:-1]]
    )
    for peer in peers:
        pl.semaphore_signal(barrier, inc=1, device_id=peer, device_id_type=MESH)

    copies = [
        pltpu.make_async_copy(cot, cot_z.at[2:34], copy_sem.at[0]),
        pltpu.make_async_copy(coarse, window.at[8:16], copy_sem.at[1]),
        pltpu.make_async_copy(first, first_v, copy_sem.at[2]),
        pltpu.make_async_copy(second, second_v, copy_sem.at[3]),
        pltpu.make_async_copy(lift, lift_v, copy_sem.at[4]),
        pltpu.make_async_copy(interp, interp_v, copy_sem.at[5]),
        pltpu.make_async_copy(fine, fine_v, copy_sem.at[6]),
    ]
    for copy in copies:
        copy.start()

    def cot_rows(row):
        return cot_z[row].astype(F32)

    zero_row = jnp.zeros((2, 128, 128), BF)
    cot_z[0:2] = zero_row
    cot_z[34:36] = zero_row
    pre_z[0:2] = zero_row
    pre_z[34:36] = zero_row
    copies[0].wait()

    def cot_step(i, carry):
        pad_cot[pl.ds(pl.multiple_of(i * PITCH, 16) + 8, 128), :] = cot_rows(i)
        shifted_row(pad_cot, x3_cot, i)
        return carry

    lax.fori_loop(2, 34, cot_step, 0)

    def fill_edges(pad, which):
        for side, columns in enumerate(((0, 1), (126, 127))):
            for j, x in enumerate(columns):
                edge_send[which, side, j] = pad[
                    pl.ds(2 * PITCH + 8 + x, 32, stride=PITCH), :
                ].astype(BF)

    fill_edges(pad_cot, 0)
    pl.semaphore_wait(barrier, len(peers))

    coarse_copies = [
        pltpu.make_async_remote_copy(
            coarse, window.at[16:24], coarse_send.at[0], coarse_recv.at[0], (up, c), MESH
        ),
        pltpu.make_async_remote_copy(
            coarse, window.at[0:8], coarse_send.at[1], coarse_recv.at[1], (down, c), MESH
        ),
    ]
    for copy in coarse_copies:
        copy.start()

    def halo_copies(which, head, tail):
        def copy(k, src, dst, device):
            return pltpu.make_async_remote_copy(
                src, dst, halo_send.at[which, k], halo_recv.at[which, k], device, MESH
            )

        edges = edge_send.at[which]
        return [
            copy(0, head, land_row.at[which, 1], (up, c)),
            copy(1, tail, land_row.at[which, 0], (down, c)),
            copy(2, edges.at[0], land_col.at[which, 1], (r, left)),
            copy(3, edges.at[1], land_col.at[which, 0], (r, right)),
            copy(4, edges.at[0, :, 0:16], land_corner.at[which, 3], (up, left)),
            copy(5, edges.at[1, :, 0:16], land_corner.at[which, 2], (up, right)),
            copy(6, edges.at[0, :, 16:32], land_corner.at[which, 1], (down, left)),
            copy(7, edges.at[1, :, 16:32], land_corner.at[which, 0], (down, right)),
        ]

    cot_halos = halo_copies(0, cot_z.at[2:4], cot_z.at[32:34])
    for copy in cot_halos:
        copy.start()

    copies[2].wait()
    copies[3].wait()
    for wp in (wp_first, wp_second, wp_first_f, wp_second_f):
        wp[1152:1536, 0:128] = jnp.zeros((384, 128), BF)
        wp[0:384, 128:256] = jnp.zeros((384, 128), BF)
    for raw, wp, wp_f in ((first_v, wp_first, wp_first_f), (second_v, wp_second, wp_second_f)):
        for a in range(3):
            for e in range(3):
                tap = raw[a, e]
                turned = raw[2 - a, 2 - e].astype(F32).T.astype(BF)
                low = a * 384 + e * 128
                for target, value in ((wp, tap), (wp_f, turned)):
                    target[low : low + 128, 0:128] = value
                    target[low + 384 : low + 512, 128:256] = value

    copies[5].wait()

    def turn(i, carry):
        slot = lax.div(i, 4)
        block = lax.rem(i, 4)
        piece = jnp.swapaxes(interp_v[slot, pl.ds(block * 32, 32)], 0, 1)
        for y in range(32):
            weights_it[pl.ds(pl.multiple_of(i * 32, 32), 32), y * 128 : (y + 1) * 128] = piece[y]
        return carry

    lax.fori_loop(0, 16, turn, 0)

    copies[1].wait()
    copies[4].wait()
    copies[6].wait()
    for copy in coarse_copies:
        copy.wait()
    local_ids = [jnp.clip(ids[k] - (r - 1) * 8, 0, 23) for k in range(4)]
    picked = jnp.concatenate([window[local_ids[k]] for k in range(4)], 1)
    mix[...] = lax.dot_general(
        picked, lift_v[...], (((0,), (0,)), ((), ())), preferred_element_type=F32
    ).astype(BF)

    def stem_step(i, carry):
        lifted = lax.dot_general(
            weights_it[:, pl.ds(pl.multiple_of(i * 512, 512), 512)],
            mix[...],
            (((0,), (0,)), ((), ())),
            preferred_element_type=F32,
        ).reshape(4, 128, 128)
        stem = (fine_v[pl.ds(i * 4, 4)].astype(F32) + lifted).astype(BF)
        stem_v[pl.ds(i * 4, 4)] = stem
        for k in range(4):
            row = i * 4 + k + 2
            pad_stem[pl.ds(pl.multiple_of(row * PITCH, 16) + 8, 128), :] = stem[k].astype(F32)
            shifted_row(pad_stem, x3_stem, row)
        return carry

    lax.fori_loop(0, 8, stem_step, 0)
    fill_edges(pad_stem, 1)
    stem_halos = halo_copies(1, stem_v.at[0:2], stem_v.at[30:32])
    for copy in stem_halos:
        copy.start()

    has_up = (r > 0).astype(F32)
    has_down = (r < n_row - 1).astype(F32)
    has_left = (c > 0).astype(F32)
    has_right = (c < n_col - 1).astype(F32)

    def take_halos(which, pad, x3):
        for side, (row, there) in enumerate(((0, has_up), (34, has_down))):
            for k in range(2):
                pad[pl.ds((row + k) * PITCH + 8, 128), :] = (
                    land_row[which, side, k].astype(F32) * there
                )
        for side, (column, there) in enumerate(((6, has_left), (136, has_right))):
            for j in range(2):
                pad[pl.ds(2 * PITCH + column + j, 32, stride=PITCH), :] = (
                    land_col[which, side, j].astype(F32) * there
                )
        for corner in range(4):
            low, side = divmod(corner, 2)
            there = (has_up, has_down)[low] * (has_left, has_right)[side]
            for j in range(2):
                tile = land_corner[which, corner, j].astype(F32) * there
                for k in range(2):
                    source = k if low else 14 + k
                    row = 34 + k if low else k
                    column = (6, 136)[side] + j
                    pad[pl.ds(row * PITCH + column, 1), :] = tile[source : source + 1]
        for row in (0, 1, 34, 35):
            shifted_row(pad, x3, row)

        def patch(row, carry):
            base = pl.multiple_of(row * 128, 128)
            start = row * PITCH + 8
            x3[pl.ds(base, 16), 0:128] = pad[pl.ds(start - 1, 16), :].astype(BF)
            x3[pl.ds(base + 112, 16), 256:384] = pad[pl.ds(start + 113, 16), :].astype(BF)
            return carry

        lax.fori_loop(2, 34, patch, 0)

    for copy in cot_halos:
        copy.wait()
    take_halos(0, pad_cot, x3_cot)
    side_grad = side_conv(pad_cot, wp_second_f)
    parts = ((0, 9), (9, 8))
    for begin, pairs in parts:
        pair = pair_conv(x3_cot, wp_second_f, 2 * begin, pairs)
        for p in range(pairs):
            for k in range(2):
                grad_act[rows_of(2 * (begin + p) + k), :] = pair[
                    p * 128 : (p + 1) * 128, k * 128 : (k + 1) * 128
                ]

    for copy in stem_halos:
        copy.wait()
    take_halos(1, pad_stem, x3_stem)

    side_act, side_pre = gate(side_conv(pad_stem, wp_first), side_grad)
    for side, (column, there) in enumerate(((7, has_left), (136, has_right))):
        where = pl.ds(PITCH + column, 40, stride=PITCH)
        pad_act[where, :] = side_act[side * 40 : side * 40 + 40] * there
        pad_pre[where, :] = side_pre[side * 40 : side * 40 + 40] * there
    for begin, pairs in parts:
        pair = pair_conv(x3_stem, wp_first, 2 * begin, pairs)
        for p in range(pairs):
            for k in range(2):
                row = 2 * (begin + p) + k
                act, pre = gate(
                    pair[p * 128 : (p + 1) * 128, k * 128 : (k + 1) * 128],
                    grad_act[rows_of(row), :],
                )
                where = pl.ds((row + 1) * PITCH + 8, 128)
                pad_act[where, :] = act
                pad_pre[where, :] = pre
                pre_z[row + 1] = pre.astype(BF)

    blank = jnp.zeros((PITCH, 128), F32)

    @pl.when(r == 0)
    def _():
        pad_act[pl.ds(PITCH, PITCH), :] = blank
        pad_pre[pl.ds(PITCH, PITCH), :] = blank

    @pl.when(r == n_row - 1)
    def _():
        pad_act[pl.ds(34 * PITCH, PITCH), :] = blank
        pad_pre[pl.ds(34 * PITCH, PITCH), :] = blank

    pre_z[1] = jnp.zeros((128, 128), BF)
    pre_z[34] = jnp.zeros((128, 128), BF)

    def shift_step(row, carry):
        shifted_row(pad_act, x3_act, row)
        shifted_row(pad_pre, x3_pre, row)
        return carry

    lax.fori_loop(1, 35, shift_step, 0)

    def tap_grad(x3, grad, group):
        total = None
        for begin, rows in ((1, 12), (13, 12), (25, 10)):
            lhs = x3[rows_of(begin, rows), :]
            rhs = jnp.concatenate(
                [
                    grad[pl.ds(begin + 1 - a, rows)].reshape(rows * 128, 128)
                    for a in range(3)
                ],
                1,
            )
            part = lax.dot_general(
                lhs, rhs, (((0,), (0,)), ((), ())), preferred_element_type=F32
            )
            if begin == 1:
                taps[...] = part
            else:
                taps[...] += part
        for a in range(3):
            local[group, a * 384 : (a + 1) * 384] = taps[:, a * 128 : (a + 1) * 128].astype(BF)

    half_rows = nq * CHUNK

    def step0(group):
        return pltpu.make_async_remote_copy(
            local.at[group, pl.ds(pl.multiple_of((1 - h) * half_rows, 16), half_rows)],
            land0.at[group],
            s0_send.at[group],
            s0_recv.at[group],
            (r, sibling),
            MESH,
        )

    def step1(group):
        return [
            pltpu.make_async_remote_copy(
                half.at[group, peer],
                land1.at[group, q],
                s1_send.at[group, peer],
                s1_recv.at[group, q],
                (r, 2 * peer + h),
                MESH,
            )
            for peer in q_peers
        ]

    def step2(group):
        return [
            pltpu.make_async_remote_copy(
                land2.at[group, r],
                land2.at[group, r],
                s2_send.at[group, peer],
                s2_recv.at[group, r],
                (peer, c),
                MESH,
            )
            for peer in r_peers
        ]

    def step3(group):
        return [
            pltpu.make_async_remote_copy(
                final.at[group, own],
                final.at[group, own],
                s3_send.at[group, peer],
                s3_recv.at[group, q],
                (r, 2 * peer + h),
                MESH,
            )
            for peer in q_peers
        ]

    def step4(group):
        mine = final.at[group, pl.ds(h * nq, nq)]
        return pltpu.make_async_remote_copy(
            mine, mine, s4_send.at[group], s4_recv.at[group], (r, sibling), MESH
        )

    def await_slots(land, sem, slots, where):
        for slot in slots:
            pltpu.make_async_remote_copy(
                land.at[where(slot)], land.at[where(slot)], sem.at[slot], sem.at[slot],
                (r, sibling), MESH,
            ).wait_recv()

    def start_all(copies):
        for copy in copies:
            copy.start()

    def end_step0(group, copy):
        copy.wait()
        for k in range(nq):
            mine = local[
                group, pl.ds(pl.multiple_of(h * half_rows + k * CHUNK, 16), CHUNK)
            ].astype(F32)
            theirs = land0[group, k * CHUNK : (k + 1) * CHUNK].astype(F32)
            half[group, k] = (mine + theirs).astype(BF)
        sends = step1(group)
        start_all(sends)
        return sends

    def end_step1(group, sends):
        await_slots(land1.at[group], s1_recv.at[group], q_peers, lambda s: s)
        land1[group, q] = half[group, q]
        total = land1[group, 0].astype(F32)
        for k in range(1, nq):
            total = total + land1[group, k].astype(F32)
        land2[group, r] = total.astype(BF)
        for copy in sends:
            copy.wait_send()
        sends = step2(group)
        start_all(sends)
        return sends

    def end_step2(group, sends):
        await_slots(land2.at[group], s2_recv.at[group], r_peers, lambda s: s)
        if group < 2:
            total = land2[group, 0].astype(F32)
            for k in range(1, n_row):
                total = total + land2[group, k].astype(F32)
            final[group, own] = (total * (1.0 / 1024.0)).astype(BF)
        else:
            total = land2[group, 0, 48:80].astype(F32)
            for k in range(1, n_row):
                total = total + land2[group, k, 48:80].astype(F32)
            lift_wide[...] = total * (1.0 / 1024.0)
            owned = (
                land2[group, r, 16:32].astype(F32)
                + land2[group, up, 32:48].astype(F32) * has_up
                + land2[group, down, 0:16].astype(F32) * has_down
            )
            final[group, own, 0:16] = owned.astype(BF)
            final[group, own, 16:80] = jnp.zeros((64, 128), BF)
        for copy in sends:
            copy.wait_send()
        sends = step3(group)
        start_all(sends)
        return sends

    def end_step3(group, sends):
        await_slots(final.at[group], s3_recv.at[group], q_peers, lambda s: h * nq + s)
        for copy in sends:
            copy.wait_send()
        copy = step4(group)
        copy.start()
        return copy

    def end_step4(group, copy):
        copy.wait_send()
        theirs = final.at[group, pl.ds((1 - h) * nq, nq)]
        pltpu.make_async_remote_copy(
            theirs, theirs, s4_send.at[group], s4_recv.at[group], (r, sibling), MESH
        ).wait_recv()

    tap_grad(x3_act, cot_z, 0)
    pend_a = step0(0)
    pend_a.start()
    tap_grad(x3_stem, pre_z, 1)
    pend_a = end_step0(0, pend_a)
    pend_b = step0(1)
    pend_b.start()

    for part in range(2):
        pair = pair_conv(x3_pre, wp_first_f, 1 + 16 * part, 8)
        for p in range(8):
            for k in range(2):
                row = 16 * part + 2 * p + k
                gf_v[row] = (
                    pair[p * 128 : (p + 1) * 128, k * 128 : (k + 1) * 128] + cot_rows(row + 2)
                ).astype(BF)
    gf_copy = pltpu.make_async_copy(gf_v, grad_fine, out_sem.at[0])
    gf_copy.start()
    pend_a = end_step1(0, pend_a)
    pend_b = end_step0(1, pend_b)

    moment = jnp.zeros((512, 128), F32)
    for part in range(4):
        moment = moment + jnp.dot(
            weights_it[:, part * 1024 : (part + 1) * 1024],
            gf_v[part * 8 : part * 8 + 8].reshape(1024, 128),
            preferred_element_type=F32,
        )
    high = moment.astype(BF)
    rest = (moment - high.astype(F32)).astype(BF)
    lift_part = jnp.dot(picked, high, preferred_element_type=F32) + jnp.dot(
        picked, rest, preferred_element_type=F32
    )
    across = (((1,), (1,)), ((), ()))
    blocks = lax.dot_general(
        lift_v[...], high, across, preferred_element_type=F32
    ) + lax.dot_general(lift_v[...], rest, across, preferred_element_type=F32)
    lift_part = lift_part.astype(BF)
    for section in range(3):
        for n in range(8):
            value = jnp.zeros((32, 128), F32)
            for k in range(4):
                value = value + jnp.where(
                    local_ids[k] == section * 8 + n, blocks[:, k * 128 : (k + 1) * 128], 0.0
                )
            value = value.astype(BF)
            for side in range(2):
                low = (2 * n + side) * CHUNK + section * 16
                local[2, low : low + 16] = value[side * 16 : side * 16 + 16]
    for owner in range(n_col):
        local[2, owner * CHUNK + 48 : owner * CHUNK + 80] = lift_part
    pend_c = step0(2)
    pend_c.start()
    pend_a = end_step2(0, pend_a)
    pend_b = end_step1(1, pend_b)

    for part in range(2):
        pair = pair_conv(x3_act, wp_second, 1 + 16 * part, 8)
        for p in range(8):
            for k in range(2):
                row = 16 * part + 2 * p + k
                out_v[row] = (
                    pair[p * 128 : (p + 1) * 128, k * 128 : (k + 1) * 128]
                    + stem_v[row].astype(F32)
                ).astype(BF)
        if part == 0:
            pend_c = end_step0(2, pend_c)
    out_copy = pltpu.make_async_copy(out_v, out, out_sem.at[1])
    out_copy.start()

    pend_a = end_step3(0, pend_a)
    pend_b = end_step2(1, pend_b)
    pend_c = end_step1(2, pend_c)
    end_step4(0, pend_a)

    def widen(group, target, sem):
        for a in range(3):
            for e in range(3):
                for part in range(8):
                    low = (a * 3 + e) * 128 + part * 16
                    owner, at = divmod(low, CHUNK)
                    wide[group, a, e, part * 16 : part * 16 + 16] = final[
                        group, owner, at : at + 16
                    ].astype(F32)
        copy = pltpu.make_async_copy(wide.at[group], target, sem)
        copy.start()
        return copy

    wide_a = widen(0, grad_second, out_sem.at[2])
    pend_b = end_step3(1, pend_b)
    pend_c = end_step2(2, pend_c)
    lift_copy = pltpu.make_async_copy(lift_wide, grad_lift, out_sem.at[3])
    lift_copy.start()
    end_step4(1, pend_b)
    wide_b = widen(1, grad_first, out_sem.at[4])
    pend_c = end_step3(2, pend_c)
    end_step4(2, pend_c)
    for n in range(8):
        for side in range(2):
            coarse_wide[n, side * 16 : side * 16 + 16] = final[2, 2 * n + side, 0:16].astype(F32)
    coarse_copy = pltpu.make_async_copy(coarse_wide, grad_coarse, out_sem.at[5])
    coarse_copy.start()
    for copy in (gf_copy, out_copy, wide_a, lift_copy, wide_b, coarse_copy):
        copy.wait()


def body(n_row, n_col, fine, coarse, block_map, interp, lift, first, second, cot):
    anywhere = pl.BlockSpec(memory_space=pl.ANY)
    nq = n_col // 2
    dma = pltpu.SemaphoreType.DMA

    def vm(shape, dtype=BF):
        return pltpu.VMEM(shape, dtype)

    pad = vm((42 * PITCH, 128), F32)
    x3 = vm((36 * 128, 384))
    wp = vm((1536, 256))
    tile = vm((32, 128, 128))
    scratch = [
        tile,
        vm((4, 128, 32, 128)),
        vm((512, 4096)),
        vm((24, 32, 128)),
        vm((32, 128)),
        vm((3, 3, 128, 128)),
        vm((3, 3, 128, 128)),
        wp, wp, wp, wp,
        pad, pad, pad, pad,
        x3, x3, x3, x3,
        vm((36, 128, 128)),
        vm((36, 128, 128)),
        tile,
        vm((34 * 128, 128), F32),
        tile,
        tile,
        vm((512, 128)),
        vm((2, 2, 2, 32, 128)),
        vm((2, 2, 2, 128, 128)),
        vm((2, 2, 2, 32, 128)),
        vm((2, 4, 2, 16, 128)),
        vm((384, 384), F32),
        vm((3, n_col * CHUNK, 128)),
        vm((3, nq * CHUNK, 128)),
        vm((3, nq, CHUNK, 128)),
        vm((3, nq, CHUNK, 128)),
        vm((3, n_row, CHUNK, 128)),
        vm((3, n_col, CHUNK, 128)),
        vm((2, 3, 3, 128, 128), F32),
        vm((8, 32, 128), F32),
        vm((32, 128), F32),
        dma((7,)), dma((6,)),
        dma((2,)), dma((2,)),
        dma((2, 8)), dma((2, 8)),
        dma((3,)), dma((3,)),
        dma((3, nq)), dma((3, nq)),
        dma((3, n_row)), dma((3, n_row)),
        dma((3, nq)), dma((3, nq)),
        dma((3,)), dma((3,)),
    ]
    shapes = (
        jax.ShapeDtypeStruct(fine.shape, BF),
        jax.ShapeDtypeStruct(fine.shape, BF),
        jax.ShapeDtypeStruct(coarse.shape, F32),
        jax.ShapeDtypeStruct(first.shape, F32),
        jax.ShapeDtypeStruct(second.shape, F32),
        jax.ShapeDtypeStruct(lift.shape, F32),
    )
    return pl.pallas_call(
        functools.partial(kernel, n_row, n_col),
        out_shape=shapes,
        in_specs=[
            anywhere, anywhere, pl.BlockSpec(memory_space=pltpu.SMEM),
            anywhere, anywhere, anywhere, anywhere, anywhere,
        ],
        out_specs=tuple([anywhere] * 6),
        scratch_shapes=scratch,
        compiler_params=pltpu.CompilerParams(
            collective_id=0, has_side_effects=True, vmem_limit_bytes=62 * 1024 * 1024
        ),
        name="step",
    )(fine, coarse, block_map.reshape(-1), interp, lift, first, second, cot)


def solution(mesh):
    n_row, n_col = mesh.shape["row"], mesh.shape["col"]
    return jax.shard_map(
        functools.partial(body, n_row, n_col),
        mesh=mesh,
        in_specs=(
            P("row", "col", None),
            P("row", None, None),
            P("row", "col", None),
            P(None, None, "row", "col"),
            P(),
            P(),
            P(),
            P("row", "col", None),
        ),
        out_specs=(
            P("row", "col", None),
            P("row", "col", None),
            P("row", None, None),
            P(),
            P(),
            P(),
        ),
        check_vma=False,
    )
```

```python
import functools

import jax
import jax.numpy as jnp
from jax import lax
from jax.experimental import pallas as pl
from jax.experimental.pallas import tpu as pltpu
from jax.sharding import PartitionSpec as P

MESH = pl.DeviceIdType.MESH
BF = jnp.bfloat16
F32 = jnp.float32
PITCH = 144
CHUNK = 80


def rows_of(row, count=1, pitch=128):
    start = row * pitch
    if not isinstance(start, int):
        start = pl.multiple_of(start, pitch if pitch == 128 else 16)
    return pl.ds(start, count * pitch)


def pair_conv(x3, wp, first, pairs):
    parts = []
    for j in range(4):
        parts.append(
            jnp.concatenate([x3[rows_of(first + 2 * p + j), :] for p in range(pairs)], 0)
        )
    return jnp.dot(jnp.concatenate(parts, 1), wp[...], preferred_element_type=F32)


def side_conv(pad, wp):
    sides = []
    for base in (6, 135):
        sides.append(
            jnp.concatenate(
                [
                    pad[pl.ds(a * PITCH + base + e, 40, stride=PITCH), :].astype(BF)
                    for a in range(3)
                    for e in range(3)
                ],
                1,
            )
        )
    return jnp.dot(
        jnp.concatenate(sides, 0), wp[0:1152, 0:128], preferred_element_type=F32
    )


def shifted_row(pad, x3, row):
    start = row * PITCH + 8
    for e in range(3):
        x3[rows_of(row), e * 128 : (e + 1) * 128] = pad[pl.ds(start + e - 1, 128), :].astype(BF)


def gate(pre, grad):
    s = 0.5 * (1.0 + jnp.tanh(0.5 * pre))
    return pre * s, grad * (s * (1.0 + pre * (1.0 - s)))


def kernel(
    n_row,
    n_col,
    fine,
    coarse,
    ids,
    interp,
    lift,
    first,
    second,
    cot,
    out,
    grad_fine,
    grad_coarse,
    grad_first,
    grad_second,
    grad_lift,
    fine_v,
    interp_v,
    weights_it,
    window,
    lift_v,
    first_v,
    second_v,
    wp_first,
    wp_second,
    wp_first_f,
    wp_second_f,
    pad_cot,
    pad_stem,
    pad_act,
    pad_pre,
    x3_cot,
    x3_stem,
    x3_act,
    x3_pre,
    cot_z,
    pre_z,
    stem_v,
    grad_act,
    mix,
    edge_send,
    land_row,
    land_col,
    land_corner,
    taps,
    local,
    land0,
    half,
    land1,
    land2,
    final,
    copy_sem,
    coarse_send,
    coarse_recv,
    halo_send,
    halo_recv,
    s0_send,
    s0_recv,
    s1_send,
    s1_recv,
    s2_send,
    s2_recv,
    s3_send,
    s3_recv,
    s4_send,
    s4_recv,
):
    r = lax.axis_index("row")
    c = lax.axis_index("col")
    nq = n_col // 2
    q = lax.div(c, 2)
    h = lax.rem(c, 2)
    sibling = c + 1 - 2 * h
    own = h * nq + q
    up = lax.rem(r + n_row - 1, n_row)
    down = lax.rem(r + 1, n_row)
    left = lax.rem(c + n_col - 1, n_col)
    right = lax.rem(c + 1, n_col)
    q_peers = [lax.rem(q + d, nq) for d in range(1, nq)]
    r_peers = [lax.rem(r + d, n_row) for d in range(1, n_row)]

    around = [
        (up, c), (down, c), (r, left), (r, right),
        (up, left), (up, right), (down, left), (down, right),
    ]
    barrier = pltpu.get_barrier_semaphore()
    peers = (
        around
        + [(r, 2 * peer + h) for peer in q_peers]
        + [(peer, c) for peer in r_peers[1:-1]]
    )
    for peer in peers:
        pl.semaphore_signal(barrier, inc=1, device_id=peer, device_id_type=MESH)

    copies = [
        pltpu.make_async_copy(cot, cot_z.at[2:34], copy_sem.at[0]),
        pltpu.make_async_copy(coarse, window.at[8:16], copy_sem.at[1]),
        pltpu.make_async_copy(first, first_v, copy_sem.at[2]),
        pltpu.make_async_copy(second, second_v, copy_sem.at[3]),
        pltpu.make_async_copy(lift, lift_v, copy_sem.at[4]),
        pltpu.make_async_copy(interp, interp_v, copy_sem.at[5]),
        pltpu.make_async_copy(fine, fine_v, copy_sem.at[6]),
    ]
    for copy in copies:
        copy.start()

    def cot_rows(row):
        return cot_z[row].astype(F32)

    zero_row = jnp.zeros((2, 128, 128), BF)
    cot_z[0:2] = zero_row
    cot_z[34:36] = zero_row
    pre_z[0:2] = zero_row
    pre_z[34:36] = zero_row
    copies[0].wait()

    def cot_step(i, carry):
        pad_cot[pl.ds(pl.multiple_of(i * PITCH, 16) + 8, 128), :] = cot_rows(i)
        shifted_row(pad_cot, x3_cot, i)
        return carry

    lax.fori_loop(2, 34, cot_step, 0)

    def fill_edges(pad, which):
        for side, columns in enumerate(((0, 1), (126, 127))):
            for j, x in enumerate(columns):
                edge_send[which, side, j] = pad[
                    pl.ds(2 * PITCH + 8 + x, 32, stride=PITCH), :
                ].astype(BF)

    fill_edges(pad_cot, 0)
    pl.semaphore_wait(barrier, len(peers))

    coarse_copies = [
        pltpu.make_async_remote_copy(
            coarse, window.at[16:24], coarse_send.at[0], coarse_recv.at[0], (up, c), MESH
        ),
        pltpu.make_async_remote_copy(
            coarse, window.at[0:8], coarse_send.at[1], coarse_recv.at[1], (down, c), MESH
        ),
    ]
    for copy in coarse_copies:
        copy.start()

    def halo_copies(which, head, tail):
        def copy(k, src, dst, device):
            return pltpu.make_async_remote_copy(
                src, dst, halo_send.at[which, k], halo_recv.at[which, k], device, MESH
            )

        edges = edge_send.at[which]
        return [
            copy(0, head, land_row.at[which, 1], (up, c)),
            copy(1, tail, land_row.at[which, 0], (down, c)),
            copy(2, edges.at[0], land_col.at[which, 1], (r, left)),
            copy(3, edges.at[1], land_col.at[which, 0], (r, right)),
            copy(4, edges.at[0, :, 0:16], land_corner.at[which, 3], (up, left)),
            copy(5, edges.at[1, :, 0:16], land_corner.at[which, 2], (up, right)),
            copy(6, edges.at[0, :, 16:32], land_corner.at[which, 1], (down, left)),
            copy(7, edges.at[1, :, 16:32], land_corner.at[which, 0], (down, right)),
        ]

    cot_halos = halo_copies(0, cot_z.at[2:4], cot_z.at[32:34])
    for copy in cot_halos:
        copy.start()

    copies[2].wait()
    copies[3].wait()
    for wp in (wp_first, wp_second, wp_first_f, wp_second_f):
        wp[1152:1536, 0:128] = jnp.zeros((384, 128), BF)
        wp[0:384, 128:256] = jnp.zeros((384, 128), BF)
    for raw, wp, wp_f in ((first_v, wp_first, wp_first_f), (second_v, wp_second, wp_second_f)):
        for a in range(3):
            for e in range(3):
                tap = raw[a, e]
                turned = raw[2 - a, 2 - e].astype(F32).T.astype(BF)
                low = a * 384 + e * 128
                for target, value in ((wp, tap), (wp_f, turned)):
                    target[low : low + 128, 0:128] = value
                    target[low + 384 : low + 512, 128:256] = value

    copies[5].wait()

    def turn(i, carry):
        slot = lax.div(i, 4)
        block = lax.rem(i, 4)
        piece = jnp.swapaxes(interp_v[slot, pl.ds(block * 32, 32)], 0, 1)
        for y in range(32):
            weights_it[pl.ds(pl.multiple_of(i * 32, 32), 32), y * 128 : (y + 1) * 128] = piece[y]
        return carry

    lax.fori_loop(0, 16, turn, 0)

    copies[1].wait()
    copies[4].wait()
    copies[6].wait()
    for copy in coarse_copies:
        copy.wait()
    local_ids = [jnp.clip(ids[k] - (r - 1) * 8, 0, 23) for k in range(4)]
    picked = jnp.concatenate([window[local_ids[k]] for k in range(4)], 1)
    mix[...] = lax.dot_general(
        picked, lift_v[...], (((0,), (0,)), ((), ())), preferred_element_type=F32
    ).astype(BF)

    def stem_step(i, carry):
        lifted = lax.dot_general(
            weights_it[:, pl.ds(pl.multiple_of(i * 512, 512), 512)],
            mix[...],
            (((0,), (0,)), ((), ())),
            preferred_element_type=F32,
        ).reshape(4, 128, 128)
        stem = (fine_v[pl.ds(i * 4, 4)].astype(F32) + lifted).astype(BF)
        stem_v[pl.ds(i * 4, 4)] = stem
        for k in range(4):
            row = i * 4 + k + 2
            pad_stem[pl.ds(pl.multiple_of(row * PITCH, 16) + 8, 128), :] = stem[k].astype(F32)
            shifted_row(pad_stem, x3_stem, row)
        return carry

    lax.fori_loop(0, 8, stem_step, 0)
    fill_edges(pad_stem, 1)
    stem_halos = halo_copies(1, stem_v.at[0:2], stem_v.at[30:32])
    for copy in stem_halos:
        copy.start()

    has_up = (r > 0).astype(F32)
    has_down = (r < n_row - 1).astype(F32)
    has_left = (c > 0).astype(F32)
    has_right = (c < n_col - 1).astype(F32)

    def take_halos(which, pad, x3):
        for side, (row, there) in enumerate(((0, has_up), (34, has_down))):
            for k in range(2):
                pad[pl.ds((row + k) * PITCH + 8, 128), :] = (
                    land_row[which, side, k].astype(F32) * there
                )
        for side, (column, there) in enumerate(((6, has_left), (136, has_right))):
            for j in range(2):
                pad[pl.ds(2 * PITCH + column + j, 32, stride=PITCH), :] = (
                    land_col[which, side, j].astype(F32) * there
                )
        for corner in range(4):
            low, side = divmod(corner, 2)
            there = (has_up, has_down)[low] * (has_left, has_right)[side]
            for j in range(2):
                tile = land_corner[which, corner, j].astype(F32) * there
                for k in range(2):
                    source = k if low else 14 + k
                    row = 34 + k if low else k
                    column = (6, 136)[side] + j
                    pad[pl.ds(row * PITCH + column, 1), :] = tile[source : source + 1]
        for row in (0, 1, 34, 35):
            shifted_row(pad, x3, row)

        def patch(row, carry):
            base = pl.multiple_of(row * 128, 128)
            start = row * PITCH + 8
            x3[pl.ds(base, 16), 0:128] = pad[pl.ds(start - 1, 16), :].astype(BF)
            x3[pl.ds(base + 112, 16), 256:384] = pad[pl.ds(start + 113, 16), :].astype(BF)
            return carry

        lax.fori_loop(2, 34, patch, 0)

    for copy in cot_halos:
        copy.wait()
    take_halos(0, pad_cot, x3_cot)
    side_grad = side_conv(pad_cot, wp_second_f)
    parts = ((0, 9), (9, 8))
    for begin, pairs in parts:
        pair = pair_conv(x3_cot, wp_second_f, 2 * begin, pairs)
        for p in range(pairs):
            for k in range(2):
                grad_act[rows_of(2 * (begin + p) + k), :] = pair[
                    p * 128 : (p + 1) * 128, k * 128 : (k + 1) * 128
                ]

    for copy in stem_halos:
        copy.wait()
    take_halos(1, pad_stem, x3_stem)

    side_act, side_pre = gate(side_conv(pad_stem, wp_first), side_grad)
    for side, (column, there) in enumerate(((7, has_left), (136, has_right))):
        where = pl.ds(PITCH + column, 40, stride=PITCH)
        pad_act[where, :] = side_act[side * 40 : side * 40 + 40] * there
        pad_pre[where, :] = side_pre[side * 40 : side * 40 + 40] * there
    for begin, pairs in parts:
        pair = pair_conv(x3_stem, wp_first, 2 * begin, pairs)
        for p in range(pairs):
            for k in range(2):
                row = 2 * (begin + p) + k
                act, pre = gate(
                    pair[p * 128 : (p + 1) * 128, k * 128 : (k + 1) * 128],
                    grad_act[rows_of(row), :],
                )
                where = pl.ds((row + 1) * PITCH + 8, 128)
                pad_act[where, :] = act
                pad_pre[where, :] = pre
                pre_z[row + 1] = pre.astype(BF)

    blank = jnp.zeros((PITCH, 128), F32)

    @pl.when(r == 0)
    def _():
        pad_act[pl.ds(PITCH, PITCH), :] = blank
        pad_pre[pl.ds(PITCH, PITCH), :] = blank

    @pl.when(r == n_row - 1)
    def _():
        pad_act[pl.ds(34 * PITCH, PITCH), :] = blank
        pad_pre[pl.ds(34 * PITCH, PITCH), :] = blank

    pre_z[1] = jnp.zeros((128, 128), BF)
    pre_z[34] = jnp.zeros((128, 128), BF)

    def shift_step(row, carry):
        shifted_row(pad_act, x3_act, row)
        shifted_row(pad_pre, x3_pre, row)
        return carry

    lax.fori_loop(1, 35, shift_step, 0)

    def tap_grad(x3, grad, group):
        total = None
        for begin, rows in ((1, 12), (13, 12), (25, 10)):
            lhs = x3[rows_of(begin, rows), :]
            rhs = jnp.concatenate(
                [
                    grad[pl.ds(begin + 1 - a, rows)].reshape(rows * 128, 128)
                    for a in range(3)
                ],
                1,
            )
            part = lax.dot_general(
                lhs, rhs, (((0,), (0,)), ((), ())), preferred_element_type=F32
            )
            if begin == 1:
                taps[...] = part
            else:
                taps[...] += part
        for a in range(3):
            local[group, a * 384 : (a + 1) * 384] = taps[:, a * 128 : (a + 1) * 128].astype(BF)

    half_rows = nq * CHUNK

    def step0(group):
        return pltpu.make_async_remote_copy(
            local.at[group, pl.ds(pl.multiple_of((1 - h) * half_rows, 16), half_rows)],
            land0.at[group],
            s0_send.at[group],
            s0_recv.at[group],
            (r, sibling),
            MESH,
        )

    def step1(group):
        return [
            pltpu.make_async_remote_copy(
                half.at[group, peer],
                land1.at[group, q],
                s1_send.at[group, peer],
                s1_recv.at[group, q],
                (r, 2 * peer + h),
                MESH,
            )
            for peer in q_peers
        ]

    def step2(group):
        return [
            pltpu.make_async_remote_copy(
                land2.at[group, r],
                land2.at[group, r],
                s2_send.at[group, peer],
                s2_recv.at[group, r],
                (peer, c),
                MESH,
            )
            for peer in r_peers
        ]

    def step3(group):
        return [
            pltpu.make_async_remote_copy(
                final.at[group, own],
                final.at[group, own],
                s3_send.at[group, peer],
                s3_recv.at[group, q],
                (r, 2 * peer + h),
                MESH,
            )
            for peer in q_peers
        ]

    def step4(group):
        mine = final.at[group, pl.ds(h * nq, nq)]
        return pltpu.make_async_remote_copy(
            mine, mine, s4_send.at[group], s4_recv.at[group], (r, sibling), MESH
        )

    def await_slots(land, sem, slots, where):
        for slot in slots:
            pltpu.make_async_remote_copy(
                land.at[where(slot)], land.at[where(slot)], sem.at[slot], sem.at[slot],
                (r, sibling), MESH,
            ).wait_recv()

    def start_all(copies):
        for copy in copies:
            copy.start()

    def end_step0(group, copy):
        copy.wait()
        for k in range(nq):
            mine = local[
                group, pl.ds(pl.multiple_of(h * half_rows + k * CHUNK, 16), CHUNK)
            ].astype(F32)
            theirs = land0[group, k * CHUNK : (k + 1) * CHUNK].astype(F32)
            half[group, k] = (mine + theirs).astype(BF)
        sends = step1(group)
        start_all(sends)
        return sends

    def end_step1(group, sends):
        await_slots(land1.at[group], s1_recv.at[group], q_peers, lambda s: s)
        land1[group, q] = half[group, q]
        total = land1[group, 0].astype(F32)
        for k in range(1, nq):
            total = total + land1[group, k].astype(F32)
        land2[group, r] = total.astype(BF)
        for copy in sends:
            copy.wait_send()
        sends = step2(group)
        start_all(sends)
        return sends

    def end_step2(group, sends):
        await_slots(land2.at[group], s2_recv.at[group], r_peers, lambda s: s)
        if group < 2:
            total = land2[group, 0].astype(F32)
            for k in range(1, n_row):
                total = total + land2[group, k].astype(F32)
            final[group, own] = (total * (1.0 / 1024.0)).astype(BF)
        else:
            total = land2[group, 0, 48:80].astype(F32)
            for k in range(1, n_row):
                total = total + land2[group, k, 48:80].astype(F32)
            grad_lift[...] = total * (1.0 / 1024.0)
            owned = (
                land2[group, r, 16:32].astype(F32)
                + land2[group, up, 32:48].astype(F32) * has_up
                + land2[group, down, 0:16].astype(F32) * has_down
            )
            final[group, own, 0:16] = owned.astype(BF)
            final[group, own, 16:80] = jnp.zeros((64, 128), BF)
        for copy in sends:
            copy.wait_send()
        sends = step3(group)
        start_all(sends)
        return sends

    def end_step3(group, sends):
        await_slots(final.at[group], s3_recv.at[group], q_peers, lambda s: h * nq + s)
        for copy in sends:
            copy.wait_send()
        copy = step4(group)
        copy.start()
        return copy

    def end_step4(group, copy):
        copy.wait_send()
        theirs = final.at[group, pl.ds((1 - h) * nq, nq)]
        pltpu.make_async_remote_copy(
            theirs, theirs, s4_send.at[group], s4_recv.at[group], (r, sibling), MESH
        ).wait_recv()

    tap_grad(x3_act, cot_z, 0)
    pend_a = step0(0)
    pend_a.start()
    tap_grad(x3_stem, pre_z, 1)
    pend_a = end_step0(0, pend_a)
    pend_b = step0(1)
    pend_b.start()

    for part in range(2):
        pair = pair_conv(x3_pre, wp_first_f, 1 + 16 * part, 8)
        for p in range(8):
            for k in range(2):
                row = 16 * part + 2 * p + k
                grad_fine[row] = (
                    pair[p * 128 : (p + 1) * 128, k * 128 : (k + 1) * 128] + cot_rows(row + 2)
                ).astype(BF)
    pend_a = end_step1(0, pend_a)
    pend_b = end_step0(1, pend_b)

    moment = jnp.zeros((512, 128), F32)
    for part in range(4):
        moment = moment + jnp.dot(
            weights_it[:, part * 1024 : (part + 1) * 1024],
            grad_fine[part * 8 : part * 8 + 8].reshape(1024, 128),
            preferred_element_type=F32,
        )
    high = moment.astype(BF)
    rest = (moment - high.astype(F32)).astype(BF)
    lift_part = jnp.dot(picked, high, preferred_element_type=F32) + jnp.dot(
        picked, rest, preferred_element_type=F32
    )
    across = (((1,), (1,)), ((), ()))
    blocks = lax.dot_general(
        lift_v[...], high, across, preferred_element_type=F32
    ) + lax.dot_general(lift_v[...], rest, across, preferred_element_type=F32)
    lift_part = lift_part.astype(BF)
    for section in range(3):
        for n in range(8):
            value = jnp.zeros((32, 128), F32)
            for k in range(4):
                value = value + jnp.where(
                    local_ids[k] == section * 8 + n, blocks[:, k * 128 : (k + 1) * 128], 0.0
                )
            value = value.astype(BF)
            for side in range(2):
                low = (2 * n + side) * CHUNK + section * 16
                local[2, low : low + 16] = value[side * 16 : side * 16 + 16]
    for owner in range(n_col):
        local[2, owner * CHUNK + 48 : owner * CHUNK + 80] = lift_part
    pend_c = step0(2)
    pend_c.start()
    pend_a = end_step2(0, pend_a)
    pend_b = end_step1(1, pend_b)

    for part in range(2):
        pair = pair_conv(x3_act, wp_second, 1 + 16 * part, 8)
        for p in range(8):
            for k in range(2):
                row = 16 * part + 2 * p + k
                out[row] = (
                    pair[p * 128 : (p + 1) * 128, k * 128 : (k + 1) * 128]
                    + stem_v[row].astype(F32)
                ).astype(BF)
        if part == 0:
            pend_c = end_step0(2, pend_c)

    pend_a = end_step3(0, pend_a)
    pend_b = end_step2(1, pend_b)
    pend_c = end_step1(2, pend_c)
    end_step4(0, pend_a)

    def widen(group, target):
        for a in range(3):
            for e in range(3):
                for part in range(8):
                    low = (a * 3 + e) * 128 + part * 16
                    owner, at = divmod(low, CHUNK)
                    target[a, e, part * 16 : part * 16 + 16] = final[
                        group, owner, at : at + 16
                    ].astype(F32)

    widen(0, grad_second)
    pend_b = end_step3(1, pend_b)
    pend_c = end_step2(2, pend_c)
    end_step4(1, pend_b)
    widen(1, grad_first)
    pend_c = end_step3(2, pend_c)
    end_step4(2, pend_c)
    for n in range(8):
        for side in range(2):
            grad_coarse[n, side * 16 : side * 16 + 16] = final[2, 2 * n + side, 0:16].astype(F32)


def hand_over(*refs):
    sems = refs[12]
    copies = []
    for k in range(6):
        source, target = refs[k], refs[6 + k]
        pieces = 4 if k < 2 else 1
        size = source.shape[0] // pieces
        for p in range(pieces):
            part = pl.ds(p * size, size)
            copies.append(pltpu.make_async_copy(source.at[part], target.at[part], sems.at[k, p]))
    for copy in copies:
        copy.start()
    for copy in copies:
        copy.wait()


def body(n_row, n_col, fine, coarse, block_map, interp, lift, first, second, cot):
    anywhere = pl.BlockSpec(memory_space=pl.ANY)
    nq = n_col // 2
    dma = pltpu.SemaphoreType.DMA

    def vm(shape, dtype=BF):
        return pltpu.VMEM(shape, dtype)

    pad = vm((42 * PITCH, 128), F32)
    x3 = vm((36 * 128, 384))
    wp = vm((1536, 256))
    tile = vm((32, 128, 128))
    scratch = [
        tile,
        vm((4, 128, 32, 128)),
        vm((512, 4096)),
        vm((24, 32, 128)),
        vm((32, 128)),
        vm((3, 3, 128, 128)),
        vm((3, 3, 128, 128)),
        wp, wp, wp, wp,
        pad, pad, pad, pad,
        x3, x3, x3, x3,
        vm((36, 128, 128)),
        vm((36, 128, 128)),
        tile,
        vm((34 * 128, 128), F32),
        vm((512, 128)),
        vm((2, 2, 2, 32, 128)),
        vm((2, 2, 2, 128, 128)),
        vm((2, 2, 2, 32, 128)),
        vm((2, 4, 2, 16, 128)),
        vm((384, 384), F32),
        vm((3, n_col * CHUNK, 128)),
        vm((3, nq * CHUNK, 128)),
        vm((3, nq, CHUNK, 128)),
        vm((3, nq, CHUNK, 128)),
        vm((3, n_row, CHUNK, 128)),
        vm((3, n_col, CHUNK, 128)),
        dma((7,)),
        dma((2,)), dma((2,)),
        dma((2, 8)), dma((2, 8)),
        dma((3,)), dma((3,)),
        dma((3, nq)), dma((3, nq)),
        dma((3, n_row)), dma((3, n_row)),
        dma((3, nq)), dma((3, nq)),
        dma((3,)), dma((3,)),
    ]
    def handed(shape, dtype):
        return pltpu.VMEM(shape, dtype)

    shapes = (
        handed(fine.shape, BF),
        handed(fine.shape, BF),
        handed(coarse.shape, F32),
        handed(first.shape, F32),
        handed(second.shape, F32),
        handed(lift.shape, F32),
    )
    results = pl.pallas_call(
        functools.partial(kernel, n_row, n_col),
        out_shape=shapes,
        in_specs=[
            anywhere, anywhere, pl.BlockSpec(memory_space=pltpu.SMEM),
            anywhere, anywhere, anywhere, anywhere, anywhere,
        ],
        out_specs=tuple([pl.BlockSpec(memory_space=pltpu.VMEM)] * 6),
        scratch_shapes=scratch,
        compiler_params=pltpu.CompilerParams(
            collective_id=0, has_side_effects=True, vmem_limit_bytes=56 * 1024 * 1024
        ),
        name="step",
    )(fine, coarse, block_map.reshape(-1), interp, lift, first, second, cot)
    return pl.pallas_call(
        hand_over,
        out_shape=tuple(jax.ShapeDtypeStruct(x.shape, x.dtype) for x in results),
        in_specs=[pl.BlockSpec(memory_space=pltpu.VMEM)] * 6,
        out_specs=tuple([anywhere] * 6),
        scratch_shapes=[dma((6, 4))],
        name="hand_over",
        compiler_params=pltpu.CompilerParams(vmem_limit_bytes=1024 * 1024),
    )(*results)


def solution(mesh):
    n_row, n_col = mesh.shape["row"], mesh.shape["col"]
    return jax.shard_map(
        functools.partial(body, n_row, n_col),
        mesh=mesh,
        in_specs=(
            P("row", "col", None),
            P("row", None, None),
            P("row", "col", None),
            P(None, None, "row", "col"),
            P(),
            P(),
            P(),
            P("row", "col", None),
        ),
        out_specs=(
            P("row", "col", None),
            P("row", "col", None),
            P("row", None, None),
            P(),
            P(),
            P(),
        ),
        check_vma=False,
    )
```

```python
import functools

import jax
import jax.numpy as jnp
from jax import lax
from jax.experimental import pallas as pl
from jax.experimental.pallas import tpu as pltpu
from jax.sharding import PartitionSpec as P

MESH = pl.DeviceIdType.MESH
BF = jnp.bfloat16
F32 = jnp.float32
PITCH = 144
CHUNK = 80


def rows_of(row, count=1, pitch=128):
    start = row * pitch
    if not isinstance(start, int):
        start = pl.multiple_of(start, pitch if pitch == 128 else 16)
    return pl.ds(start, count * pitch)


def pair_conv(x3, wp, starts):
    parts = []
    for j in range(4):
        parts.append(jnp.concatenate([x3[rows_of(start + j), :] for start in starts], 0))
    return jnp.dot(jnp.concatenate(parts, 1), wp[...], preferred_element_type=F32)


SIDES = (7, 8, 135, 136)


def side_conv(pad, wp):
    sides = []
    for column in SIDES:
        sides.append(
            jnp.concatenate(
                [
                    pad[pl.ds(a * PITCH + column - 1 + e, 40, stride=PITCH), :].astype(BF)
                    for a in range(3)
                    for e in range(3)
                ],
                1,
            )
        )
    return jnp.dot(
        jnp.concatenate(sides, 0), wp[0:1152, 0:128], preferred_element_type=F32
    )


def shifted_row(pad, x3, row):
    start = row * PITCH + 8
    for e in range(3):
        x3[rows_of(row), e * 128 : (e + 1) * 128] = pad[pl.ds(start + e - 1, 128), :].astype(BF)


def gate(pre, grad):
    s = 0.5 * (1.0 + jnp.tanh(0.5 * pre))
    return pre * s, grad * (s * (1.0 + pre * (1.0 - s)))


def kernel(
    n_row,
    n_col,
    fine,
    coarse,
    ids,
    interp,
    lift,
    first,
    second,
    cot,
    out,
    grad_fine,
    grad_coarse,
    grad_first,
    grad_second,
    grad_lift,
    fine_v,
    interp_v,
    weights_it,
    window,
    lift_v,
    first_v,
    second_v,
    wp_first,
    wp_second,
    wp_first_f,
    wp_second_f,
    pad_cot,
    pad_stem,
    pad_act,
    pad_pre,
    x3_cot,
    x3_stem,
    x3_act,
    x3_pre,
    cot_z,
    pre_z,
    stem_v,
    grad_act,
    mix,
    edge_send,
    land_row,
    land_col,
    land_corner,
    taps,
    local,
    land0,
    half,
    land1,
    land2,
    final,
    copy_sem,
    coarse_send,
    coarse_recv,
    halo_send,
    halo_recv,
    s0_send,
    s0_recv,
    s1_send,
    s1_recv,
    s2_send,
    s2_recv,
    s3_send,
    s3_recv,
    s4_send,
    s4_recv,
):
    r = lax.axis_index("row")
    c = lax.axis_index("col")
    nq = n_col // 2
    q = lax.div(c, 2)
    h = lax.rem(c, 2)
    sibling = c + 1 - 2 * h
    own = h * nq + q
    up = lax.rem(r + n_row - 1, n_row)
    down = lax.rem(r + 1, n_row)
    left = lax.rem(c + n_col - 1, n_col)
    right = lax.rem(c + 1, n_col)
    q_peers = [lax.rem(q + d, nq) for d in range(1, nq)]
    r_peers = [lax.rem(r + d, n_row) for d in range(1, n_row)]

    around = [
        (up, c), (down, c), (r, left), (r, right),
        (up, left), (up, right), (down, left), (down, right),
    ]
    barrier = pltpu.get_barrier_semaphore()
    peers = (
        around
        + [(r, 2 * peer + h) for peer in q_peers]
        + [(peer, c) for peer in r_peers[1:-1]]
    )
    for peer in peers:
        pl.semaphore_signal(barrier, inc=1, device_id=peer, device_id_type=MESH)

    copies = [
        pltpu.make_async_copy(cot, cot_z.at[2:34], copy_sem.at[0]),
        pltpu.make_async_copy(coarse, window.at[8:16], copy_sem.at[1]),
        pltpu.make_async_copy(first, first_v, copy_sem.at[2]),
        pltpu.make_async_copy(second, second_v, copy_sem.at[3]),
        pltpu.make_async_copy(lift, lift_v, copy_sem.at[4]),
        pltpu.make_async_copy(fine, fine_v, copy_sem.at[5]),
    ]
    slot_copies = [
        pltpu.make_async_copy(interp.at[k], interp_v.at[k], copy_sem.at[6 + k]) for k in range(4)
    ]
    for copy in copies[0:5] + slot_copies + copies[5:6]:
        copy.start()

    zero_row = jnp.zeros((2, 128, 128), BF)
    cot_z[0:2] = zero_row
    cot_z[34:36] = zero_row
    pre_z[0:2] = zero_row
    pre_z[34:36] = zero_row

    def halo_copy(which, k, src, dst, device):
        return pltpu.make_async_remote_copy(
            src, dst, halo_send.at[which, k], halo_recv.at[which, k], device, MESH
        )

    def row_halos(which, source):
        return [
            halo_copy(which, 0, source.at[0:2], land_row.at[which, 1], (up, c)),
            halo_copy(which, 1, source.at[30:32], land_row.at[which, 0], (down, c)),
        ]

    def column_halos(which):
        edges = edge_send.at[which]
        return [
            halo_copy(which, 2, edges.at[0], land_col.at[which, 1], (r, left)),
            halo_copy(which, 3, edges.at[1], land_col.at[which, 0], (r, right)),
            halo_copy(which, 4, edges.at[0, :, 0:16], land_corner.at[which, 3], (up, left)),
            halo_copy(which, 5, edges.at[1, :, 0:16], land_corner.at[which, 2], (up, right)),
            halo_copy(which, 6, edges.at[0, :, 16:32], land_corner.at[which, 1], (down, left)),
            halo_copy(which, 7, edges.at[1, :, 16:32], land_corner.at[which, 0], (down, right)),
        ]

    pl.semaphore_wait(barrier, len(peers))
    coarse_copies = [
        pltpu.make_async_remote_copy(
            coarse, window.at[16:24], coarse_send.at[0], coarse_recv.at[0], (up, c), MESH
        ),
        pltpu.make_async_remote_copy(
            coarse, window.at[0:8], coarse_send.at[1], coarse_recv.at[1], (down, c), MESH
        ),
    ]
    cot_halos = row_halos(0, cot)
    for copy in coarse_copies + cot_halos:
        copy.start()

    def cot_rows(row):
        return cot_z[row].astype(F32)

    copies[0].wait()

    def cot_step(i, carry):
        pad_cot[pl.ds(pl.multiple_of(i * PITCH, 16) + 8, 128), :] = cot_rows(i)
        shifted_row(pad_cot, x3_cot, i)
        return carry

    lax.fori_loop(2, 34, cot_step, 0)

    def fill_edges(pad, which):
        for side, columns in enumerate(((0, 1), (126, 127))):
            for j, x in enumerate(columns):
                edge_send[which, side, j] = pad[
                    pl.ds(2 * PITCH + 8 + x, 32, stride=PITCH), :
                ].astype(BF)

    fill_edges(pad_cot, 0)
    cot_sides = column_halos(0)
    for copy in cot_sides:
        copy.start()
    cot_halos = cot_halos + cot_sides

    copies[2].wait()
    copies[3].wait()
    for wp in (wp_first, wp_second, wp_first_f, wp_second_f):
        wp[1152:1536, 0:128] = jnp.zeros((384, 128), BF)
        wp[0:384, 128:256] = jnp.zeros((384, 128), BF)
    for raw, wp, wp_f in ((first_v, wp_first, wp_first_f), (second_v, wp_second, wp_second_f)):
        for a in range(3):
            for e in range(3):
                tap = raw[a, e]
                turned = raw[2 - a, 2 - e].astype(F32).T.astype(BF)
                low = a * 384 + e * 128
                for target, value in ((wp, tap), (wp_f, turned)):
                    target[low : low + 128, 0:128] = value
                    target[low + 384 : low + 512, 128:256] = value

    inner = (tuple(range(2, 18, 2)), tuple(range(18, 32, 2)))

    def rows_of_pairs(pair, starts):
        for p, start in enumerate(starts):
            for k in range(2):
                yield start + k, pair[p * 128 : (p + 1) * 128, k * 128 : (k + 1) * 128]

    for starts in inner:
        for row, value in rows_of_pairs(pair_conv(x3_cot, wp_second_f, starts), starts):
            grad_act[rows_of(row), :] = value

    for slot in range(4):
        slot_copies[slot].wait()

        def turn(i, carry, slot=slot):
            piece = jnp.swapaxes(interp_v[slot, pl.ds(i * 32, 32)], 0, 1)
            where = pl.ds(pl.multiple_of(slot * 128 + i * 32, 32), 32)
            for y in range(32):
                weights_it[where, y * 128 : (y + 1) * 128] = piece[y]
            return carry

        lax.fori_loop(0, 4, turn, 0)

    copies[1].wait()
    copies[4].wait()
    copies[5].wait()
    for copy in coarse_copies:
        copy.wait()
    local_ids = [jnp.clip(ids[k] - (r - 1) * 8, 0, 23) for k in range(4)]
    picked = jnp.concatenate([window[local_ids[k]] for k in range(4)], 1)
    mix[...] = lax.dot_general(
        picked, lift_v[...], (((0,), (0,)), ((), ())), preferred_element_type=F32
    ).astype(BF)

    def stem_step(i, carry):
        lifted = lax.dot_general(
            weights_it[:, pl.ds(pl.multiple_of(i * 512, 512), 512)],
            mix[...],
            (((0,), (0,)), ((), ())),
            preferred_element_type=F32,
        ).reshape(4, 128, 128)
        stem = (fine_v[pl.ds(i * 4, 4)].astype(F32) + lifted).astype(BF)
        stem_v[pl.ds(i * 4, 4)] = stem
        for k in range(4):
            row = i * 4 + k + 2
            pad_stem[pl.ds(pl.multiple_of(row * PITCH, 16) + 8, 128), :] = stem[k].astype(F32)
            shifted_row(pad_stem, x3_stem, row)
        return carry

    stem_step(0, 0)
    stem_step(7, 0)
    stem_halos = row_halos(1, stem_v)
    for copy in stem_halos:
        copy.start()
    lax.fori_loop(1, 7, stem_step, 0)
    fill_edges(pad_stem, 1)
    stem_sides = column_halos(1)
    for copy in stem_sides:
        copy.start()
    stem_halos = stem_halos + stem_sides

    def put(row, act, pre):
        where = pl.ds((row + 1) * PITCH + 8, 128)
        pad_act[where, :] = act
        pad_pre[where, :] = pre

    for starts in inner:
        for row, value in rows_of_pairs(pair_conv(x3_stem, wp_first, starts), starts):
            put(row, *gate(value, grad_act[rows_of(row), :]))

    has_up = (r > 0).astype(F32)
    has_down = (r < n_row - 1).astype(F32)
    has_left = (c > 0).astype(F32)
    has_right = (c < n_col - 1).astype(F32)

    def take_halos(which, pad, x3):
        for side, (row, there) in enumerate(((0, has_up), (34, has_down))):
            for k in range(2):
                pad[pl.ds((row + k) * PITCH + 8, 128), :] = (
                    land_row[which, side, k].astype(F32) * there
                )
        for side, (column, there) in enumerate(((6, has_left), (136, has_right))):
            for j in range(2):
                pad[pl.ds(2 * PITCH + column + j, 32, stride=PITCH), :] = (
                    land_col[which, side, j].astype(F32) * there
                )
        for corner in range(4):
            low, side = divmod(corner, 2)
            there = (has_up, has_down)[low] * (has_left, has_right)[side]
            for j in range(2):
                tile = land_corner[which, corner, j].astype(F32) * there
                for k in range(2):
                    source = k if low else 14 + k
                    row = 34 + k if low else k
                    column = (6, 136)[side] + j
                    pad[pl.ds(row * PITCH + column, 1), :] = tile[source : source + 1]
        for row in (0, 1, 34, 35):
            shifted_row(pad, x3, row)

        def patch(row, carry):
            base = pl.multiple_of(row * 128, 128)
            start = row * PITCH + 8
            x3[pl.ds(base, 16), 0:128] = pad[pl.ds(start - 1, 16), :].astype(BF)
            x3[pl.ds(base + 112, 16), 256:384] = pad[pl.ds(start + 113, 16), :].astype(BF)
            return carry

        lax.fori_loop(2, 34, patch, 0)

    for copy in cot_halos:
        copy.wait()
    take_halos(0, pad_cot, x3_cot)
    outer = (0, 32)
    side_grad = side_conv(pad_cot, wp_second_f)
    for row, value in rows_of_pairs(pair_conv(x3_cot, wp_second_f, outer), outer):
        grad_act[rows_of(row), :] = value
    for copy in stem_halos:
        copy.wait()
    take_halos(1, pad_stem, x3_stem)
    for row, value in rows_of_pairs(pair_conv(x3_stem, wp_first, outer), outer):
        put(row, *gate(value, grad_act[rows_of(row), :]))
    side_act, side_pre = gate(side_conv(pad_stem, wp_first), side_grad)
    for side, (column, there) in enumerate(zip(SIDES, (has_left, 1.0, 1.0, has_right))):
        where = pl.ds(PITCH + column, 40, stride=PITCH)
        pad_act[where, :] = side_act[side * 40 : side * 40 + 40] * there
        pad_pre[where, :] = side_pre[side * 40 : side * 40 + 40] * there

    blank = jnp.zeros((PITCH, 128), F32)

    @pl.when(r == 0)
    def _():
        pad_act[pl.ds(PITCH, PITCH), :] = blank
        pad_pre[pl.ds(PITCH, PITCH), :] = blank

    @pl.when(r == n_row - 1)
    def _():
        pad_act[pl.ds(34 * PITCH, PITCH), :] = blank
        pad_pre[pl.ds(34 * PITCH, PITCH), :] = blank

    def shift_step(row, carry):
        shifted_row(pad_act, x3_act, row)
        shifted_row(pad_pre, x3_pre, row)
        return carry

    lax.fori_loop(1, 35, shift_step, 0)

    def keep_step(row, carry):
        pre_z[row] = x3_pre[pl.ds(pl.multiple_of(row * 128, 128), 128), 128:256]
        return carry

    lax.fori_loop(2, 34, keep_step, 0)

    def tap_grad(x3, grad, group):
        total = None
        for begin, rows in ((1, 12), (13, 12), (25, 10)):
            lhs = x3[rows_of(begin, rows), :]
            rhs = jnp.concatenate(
                [
                    grad[pl.ds(begin + 1 - a, rows)].reshape(rows * 128, 128)
                    for a in range(3)
                ],
                1,
            )
            part = lax.dot_general(
                lhs, rhs, (((0,), (0,)), ((), ())), preferred_element_type=F32
            )
            if begin == 1:
                taps[...] = part
            else:
                taps[...] += part
        for a in range(3):
            local[group, a * 384 : (a + 1) * 384] = taps[:, a * 128 : (a + 1) * 128].astype(BF)

    half_rows = nq * CHUNK

    def step0(group):
        return pltpu.make_async_remote_copy(
            local.at[group, pl.ds(pl.multiple_of((1 - h) * half_rows, 16), half_rows)],
            land0.at[group],
            s0_send.at[group],
            s0_recv.at[group],
            (r, sibling),
            MESH,
        )

    def step1(group):
        return [
            pltpu.make_async_remote_copy(
                half.at[group, peer],
                land1.at[group, q],
                s1_send.at[group, peer],
                s1_recv.at[group, q],
                (r, 2 * peer + h),
                MESH,
            )
            for peer in q_peers
        ]

    def step2(group):
        return [
            pltpu.make_async_remote_copy(
                land2.at[group, r],
                land2.at[group, r],
                s2_send.at[group, peer],
                s2_recv.at[group, r],
                (peer, c),
                MESH,
            )
            for peer in r_peers
        ]

    def chunk_of(group, owner):
        rows = CHUNK if group < 2 else 16
        return final.at[group, owner, 0:rows]

    def step3(group):
        mine = chunk_of(group, own)
        return [
            pltpu.make_async_remote_copy(
                mine,
                mine,
                s3_send.at[group, peer],
                s3_recv.at[group, q],
                (r, 2 * peer + h),
                MESH,
            )
            for peer in q_peers
        ]

    def step4(group, k):
        theirs = chunk_of(group, h * nq + k)
        return pltpu.make_async_remote_copy(
            theirs, theirs, s4_send.at[group, k], s4_recv.at[group, k], (r, sibling), MESH
        )

    def await_slots(land, sem, slots, where):
        for slot in slots:
            pltpu.make_async_remote_copy(
                land.at[where(slot)], land.at[where(slot)], sem.at[slot], sem.at[slot],
                (r, sibling), MESH,
            ).wait_recv()

    def start_all(copies):
        for copy in copies:
            copy.start()

    def end_step0(group, copy):
        copy.wait()
        for k in range(nq):
            mine = local[
                group, pl.ds(pl.multiple_of(h * half_rows + k * CHUNK, 16), CHUNK)
            ].astype(F32)
            theirs = land0[group, k * CHUNK : (k + 1) * CHUNK].astype(F32)
            half[group, k] = (mine + theirs).astype(BF)
        sends = step1(group)
        start_all(sends)
        return sends

    def end_step1(group, sends):
        await_slots(land1.at[group], s1_recv.at[group], q_peers, lambda s: s)
        land1[group, q] = half[group, q]
        total = land1[group, 0].astype(F32)
        for k in range(1, nq):
            total = total + land1[group, k].astype(F32)
        land2[group, r] = total.astype(BF)
        for copy in sends:
            copy.wait_send()
        sends = step2(group)
        start_all(sends)
        return sends

    def end_step2(group, sends):
        await_slots(land2.at[group], s2_recv.at[group], r_peers, lambda s: s)
        if group < 2:
            total = land2[group, 0].astype(F32)
            for k in range(1, n_row):
                total = total + land2[group, k].astype(F32)
            final[group, own] = (total * (1.0 / 1024.0)).astype(BF)
        else:
            total = land2[group, 0, 48:80].astype(F32)
            for k in range(1, n_row):
                total = total + land2[group, k, 48:80].astype(F32)
            grad_lift[...] = total * (1.0 / 1024.0)
            owned = (
                land2[group, r, 16:32].astype(F32)
                + land2[group, up, 32:48].astype(F32) * has_up
                + land2[group, down, 0:16].astype(F32) * has_down
            )
            final[group, own, 0:16] = owned.astype(BF)
        for copy in sends:
            copy.wait_send()
        sends = step3(group)
        start_all(sends)
        return sends

    def end_step3(group, sends):
        passed = [step4(group, q)]
        passed[0].start()
        for peer in reversed(q_peers):
            landed = chunk_of(group, h * nq + peer)
            pltpu.make_async_remote_copy(
                landed, landed, s3_send.at[group, peer], s3_recv.at[group, peer],
                (r, sibling), MESH,
            ).wait_recv()
            copy = step4(group, peer)
            copy.start()
            passed.append(copy)
        for copy in sends:
            copy.wait_send()
        return passed

    def end_step4(group, passed):
        for copy in passed:
            copy.wait_send()
        for k in range(nq):
            landed = chunk_of(group, (1 - h) * nq + k)
            pltpu.make_async_remote_copy(
                landed, landed, s4_send.at[group, k], s4_recv.at[group, k], (r, sibling), MESH
            ).wait_recv()

    tap_grad(x3_act, cot_z, 0)
    pend_a = step0(0)
    pend_a.start()
    tap_grad(x3_stem, pre_z, 1)
    pend_a = end_step0(0, pend_a)
    pend_b = step0(1)
    pend_b.start()

    for part in range(2):
        starts = tuple(range(1 + 16 * part, 17 + 16 * part, 2))
        pair = pair_conv(x3_pre, wp_first_f, starts)
        for p in range(8):
            for k in range(2):
                row = 16 * part + 2 * p + k
                grad_fine[row] = (
                    pair[p * 128 : (p + 1) * 128, k * 128 : (k + 1) * 128] + cot_rows(row + 2)
                ).astype(BF)
    pend_b = end_step0(1, pend_b)

    moment = jnp.zeros((512, 128), F32)
    for part in range(4):
        moment = moment + jnp.dot(
            weights_it[:, part * 1024 : (part + 1) * 1024],
            grad_fine[part * 8 : part * 8 + 8].reshape(1024, 128),
            preferred_element_type=F32,
        )
    high = moment.astype(BF)
    rest = (moment - high.astype(F32)).astype(BF)
    lift_part = jnp.dot(picked, high, preferred_element_type=F32) + jnp.dot(
        picked, rest, preferred_element_type=F32
    )
    across = (((1,), (1,)), ((), ()))
    blocks = lax.dot_general(
        lift_v[...], high, across, preferred_element_type=F32
    ) + lax.dot_general(lift_v[...], rest, across, preferred_element_type=F32)
    lift_part = lift_part.astype(BF)
    for section in range(3):
        for n in range(8):
            value = jnp.zeros((32, 128), F32)
            for k in range(4):
                value = value + jnp.where(
                    local_ids[k] == section * 8 + n, blocks[:, k * 128 : (k + 1) * 128], 0.0
                )
            value = value.astype(BF)
            for side in range(2):
                low = (2 * n + side) * CHUNK + section * 16
                local[2, low : low + 16] = value[side * 16 : side * 16 + 16]
    for owner in range(n_col):
        local[2, owner * CHUNK + 48 : owner * CHUNK + 80] = lift_part
    pend_c = step0(2)
    pend_c.start()
    pend_a = end_step1(0, pend_a)

    for part in range(2):
        starts = tuple(range(1 + 16 * part, 17 + 16 * part, 2))
        pair = pair_conv(x3_act, wp_second, starts)
        for p in range(8):
            for k in range(2):
                row = 16 * part + 2 * p + k
                out[row] = (
                    pair[p * 128 : (p + 1) * 128, k * 128 : (k + 1) * 128]
                    + stem_v[row].astype(F32)
                ).astype(BF)
        if part == 0:
            pend_c = end_step0(2, pend_c)
    pend_b = end_step1(1, pend_b)
    pend_a = end_step2(0, pend_a)
    pend_c = end_step1(2, pend_c)
    pend_b = end_step2(1, pend_b)

    def widen(group, target):
        for a in range(3):
            for e in range(3):
                for part in range(8):
                    low = (a * 3 + e) * 128 + part * 16
                    owner, at = divmod(low, CHUNK)
                    target[a, e, part * 16 : part * 16 + 16] = final[
                        group, owner, at : at + 16
                    ].astype(F32)

    pend_a = end_step3(0, pend_a)
    pend_c = end_step2(2, pend_c)
    pend_b = end_step3(1, pend_b)
    end_step4(0, pend_a)
    widen(0, grad_second)
    pend_c = end_step3(2, pend_c)
    end_step4(1, pend_b)
    widen(1, grad_first)
    end_step4(2, pend_c)
    for n in range(8):
        for side in range(2):
            grad_coarse[n, side * 16 : side * 16 + 16] = final[2, 2 * n + side, 0:16].astype(F32)


def hand_over(*refs):
    sems = refs[12]
    copies = []
    for k in range(6):
        source, target = refs[k], refs[6 + k]
        pieces = 4 if k < 2 else 1
        size = source.shape[0] // pieces
        for p in range(pieces):
            part = pl.ds(p * size, size)
            copies.append(pltpu.make_async_copy(source.at[part], target.at[part], sems.at[k, p]))
    for copy in copies:
        copy.start()
    for copy in copies:
        copy.wait()


def body(n_row, n_col, fine, coarse, block_map, interp, lift, first, second, cot):
    anywhere = pl.BlockSpec(memory_space=pl.ANY)
    nq = n_col // 2
    dma = pltpu.SemaphoreType.DMA

    def vm(shape, dtype=BF):
        return pltpu.VMEM(shape, dtype)

    pad = vm((42 * PITCH, 128), F32)
    x3 = vm((36 * 128, 384))
    wp = vm((1536, 256))
    tile = vm((32, 128, 128))
    scratch = [
        tile,
        vm((4, 128, 32, 128)),
        vm((512, 4096)),
        vm((24, 32, 128)),
        vm((32, 128)),
        vm((3, 3, 128, 128)),
        vm((3, 3, 128, 128)),
        wp, wp, wp, wp,
        pad, pad, pad, pad,
        x3, x3, x3, x3,
        vm((36, 128, 128)),
        vm((36, 128, 128)),
        tile,
        vm((34 * 128, 128), F32),
        vm((512, 128)),
        vm((2, 2, 2, 32, 128)),
        vm((2, 2, 2, 128, 128)),
        vm((2, 2, 2, 32, 128)),
        vm((2, 4, 2, 16, 128)),
        vm((384, 384), F32),
        vm((3, n_col * CHUNK, 128)),
        vm((3, nq * CHUNK, 128)),
        vm((3, nq, CHUNK, 128)),
        vm((3, nq, CHUNK, 128)),
        vm((3, n_row, CHUNK, 128)),
        vm((3, n_col, CHUNK, 128)),
        dma((10,)),
        dma((2,)), dma((2,)),
        dma((2, 8)), dma((2, 8)),
        dma((3,)), dma((3,)),
        dma((3, nq)), dma((3, nq)),
        dma((3, n_row)), dma((3, n_row)),
        dma((3, nq)), dma((3, nq)),
        dma((3, nq)), dma((3, nq)),
    ]
    def handed(shape, dtype):
        return pltpu.VMEM(shape, dtype)

    shapes = (
        handed(fine.shape, BF),
        handed(fine.shape, BF),
        handed(coarse.shape, F32),
        handed(first.shape, F32),
        handed(second.shape, F32),
        handed(lift.shape, F32),
    )
    results = pl.pallas_call(
        functools.partial(kernel, n_row, n_col),
        out_shape=shapes,
        in_specs=[
            anywhere, anywhere, pl.BlockSpec(memory_space=pltpu.SMEM),
            anywhere, anywhere, anywhere, anywhere, anywhere,
        ],
        out_specs=tuple([pl.BlockSpec(memory_space=pltpu.VMEM)] * 6),
        scratch_shapes=scratch,
        compiler_params=pltpu.CompilerParams(
            collective_id=0, has_side_effects=True, vmem_limit_bytes=56 * 1024 * 1024
        ),
        name="step",
    )(fine, coarse, block_map.reshape(-1), interp, lift, first, second, cot)
    return pl.pallas_call(
        hand_over,
        out_shape=tuple(jax.ShapeDtypeStruct(x.shape, x.dtype) for x in results),
        in_specs=[pl.BlockSpec(memory_space=pltpu.VMEM)] * 6,
        out_specs=tuple([anywhere] * 6),
        scratch_shapes=[dma((6, 4))],
        name="hand_over",
        compiler_params=pltpu.CompilerParams(vmem_limit_bytes=1024 * 1024),
    )(*results)


def solution(mesh):
    n_row, n_col = mesh.shape["row"], mesh.shape["col"]
    return jax.shard_map(
        functools.partial(body, n_row, n_col),
        mesh=mesh,
        in_specs=(
            P("row", "col", None),
            P("row", None, None),
            P("row", "col", None),
            P(None, None, "row", "col"),
            P(),
            P(),
            P(),
            P("row", "col", None),
        ),
        out_specs=(
            P("row", "col", None),
            P("row", "col", None),
            P("row", None, None),
            P(),
            P(),
            P(),
        ),
        check_vma=False,
    )
```

```python
import functools

import jax
import jax.numpy as jnp
from jax import lax
from jax.experimental import pallas as pl
from jax.experimental.pallas import tpu as pltpu
from jax.sharding import PartitionSpec as P

MESH = pl.DeviceIdType.MESH
BF = jnp.bfloat16
F32 = jnp.float32
PITCH = 144
CHUNK = 80
SIZES = (CHUNK, CHUNK, 64)


def rows_of(row, count=1, pitch=128):
    start = row * pitch
    if not isinstance(start, int):
        start = pl.multiple_of(start, pitch if pitch == 128 else 16)
    return pl.ds(start, count * pitch)


def pair_conv(x3, wp, starts):
    parts = []
    for j in range(4):
        parts.append(jnp.concatenate([x3[rows_of(start + j), :] for start in starts], 0))
    return jnp.dot(jnp.concatenate(parts, 1), wp[...], preferred_element_type=F32)


SIDES = (7, 8, 135, 136)


def side_conv(pad, wp):
    sides = []
    for column in SIDES:
        sides.append(
            jnp.concatenate(
                [
                    pad[pl.ds(a * PITCH + column - 1 + e, 40, stride=PITCH), :].astype(BF)
                    for a in range(3)
                    for e in range(3)
                ],
                1,
            )
        )
    return jnp.dot(
        jnp.concatenate(sides, 0), wp[0:1152, 0:128], preferred_element_type=F32
    )


def shifted_row(pad, x3, row):
    start = row * PITCH + 8
    for e in range(3):
        x3[rows_of(row), e * 128 : (e + 1) * 128] = pad[pl.ds(start + e - 1, 128), :].astype(BF)


def gate(pre, grad):
    s = 0.5 * (1.0 + jnp.tanh(0.5 * pre))
    return pre * s, grad * (s * (1.0 + pre * (1.0 - s)))


def kernel(
    n_row,
    n_col,
    fine,
    coarse,
    ids,
    interp,
    lift,
    first,
    second,
    cot,
    out,
    grad_fine,
    grad_coarse,
    grad_first,
    grad_second,
    grad_lift,
    fine_v,
    interp_v,
    weights_it,
    window,
    lift_v,
    first_v,
    second_v,
    wp_first,
    wp_second,
    wp_first_f,
    wp_second_f,
    pad_cot,
    pad_stem,
    pad_act,
    pad_pre,
    x3_cot,
    x3_stem,
    x3_act,
    x3_pre,
    cot_z,
    pre_z,
    stem_v,
    grad_act,
    mix,
    edge_send,
    land_row,
    land_col,
    land_corner,
    taps,
    local,
    land0,
    half,
    land1,
    land2,
    final,
    copy_sem,
    coarse_send,
    coarse_recv,
    halo_send,
    halo_recv,
    s0_send,
    s0_recv,
    s1_send,
    s1_recv,
    s2_send,
    s2_recv,
    s3_send,
    s3_recv,
    s4_send,
    s4_recv,
    blocks_send,
    blocks_recv,
    lift_send,
    lift_recv,
    lift_sum,
):
    r = lax.axis_index("row")
    c = lax.axis_index("col")
    nq = n_col // 2
    q = lax.div(c, 2)
    h = lax.rem(c, 2)
    sibling = c + 1 - 2 * h
    own = h * nq + q
    up = lax.rem(r + n_row - 1, n_row)
    down = lax.rem(r + 1, n_row)
    left = lax.rem(c + n_col - 1, n_col)
    right = lax.rem(c + 1, n_col)
    q_peers = [lax.rem(q + d, nq) for d in range(1, nq)]
    r_peers = [lax.rem(r + d, n_row) for d in range(1, n_row)]

    around = [
        (up, c), (down, c), (r, left), (r, right),
        (up, left), (up, right), (down, left), (down, right),
    ]
    barrier = pltpu.get_barrier_semaphore()
    peers = (
        around
        + [(r, 2 * peer + h) for peer in q_peers]
        + [(peer, c) for peer in r_peers[1:-1]]
    )
    for peer in peers:
        pl.semaphore_signal(barrier, inc=1, device_id=peer, device_id_type=MESH)

    copies = [
        pltpu.make_async_copy(cot, cot_z.at[2:34], copy_sem.at[0]),
        pltpu.make_async_copy(coarse, window.at[8:16], copy_sem.at[1]),
        pltpu.make_async_copy(first, first_v, copy_sem.at[2]),
        pltpu.make_async_copy(second, second_v, copy_sem.at[3]),
        pltpu.make_async_copy(lift, lift_v, copy_sem.at[4]),
        pltpu.make_async_copy(fine, fine_v, copy_sem.at[5]),
    ]
    slot_copies = [
        pltpu.make_async_copy(interp.at[k], interp_v.at[k], copy_sem.at[6 + k]) for k in range(4)
    ]
    for copy in copies[0:5] + slot_copies + copies[5:6]:
        copy.start()

    zero_row = jnp.zeros((2, 128, 128), BF)
    cot_z[0:2] = zero_row
    cot_z[34:36] = zero_row
    pre_z[0:2] = zero_row
    pre_z[34:36] = zero_row

    def halo_copy(which, k, src, dst, device):
        return pltpu.make_async_remote_copy(
            src, dst, halo_send.at[which, k], halo_recv.at[which, k], device, MESH
        )

    def row_halos(which, source):
        return [
            halo_copy(which, 0, source.at[0:2], land_row.at[which, 1], (up, c)),
            halo_copy(which, 1, source.at[30:32], land_row.at[which, 0], (down, c)),
        ]

    def column_halos(which):
        edges = edge_send.at[which]
        return [
            halo_copy(which, 2, edges.at[0], land_col.at[which, 1], (r, left)),
            halo_copy(which, 3, edges.at[1], land_col.at[which, 0], (r, right)),
            halo_copy(which, 4, edges.at[0, :, 0:16], land_corner.at[which, 3], (up, left)),
            halo_copy(which, 5, edges.at[1, :, 0:16], land_corner.at[which, 2], (up, right)),
            halo_copy(which, 6, edges.at[0, :, 16:32], land_corner.at[which, 1], (down, left)),
            halo_copy(which, 7, edges.at[1, :, 16:32], land_corner.at[which, 0], (down, right)),
        ]

    pl.semaphore_wait(barrier, len(peers))
    coarse_copies = [
        pltpu.make_async_remote_copy(
            coarse, window.at[16:24], coarse_send.at[0], coarse_recv.at[0], (up, c), MESH
        ),
        pltpu.make_async_remote_copy(
            coarse, window.at[0:8], coarse_send.at[1], coarse_recv.at[1], (down, c), MESH
        ),
    ]
    cot_halos = row_halos(0, cot)
    for copy in coarse_copies + cot_halos:
        copy.start()

    def cot_rows(row):
        return cot_z[row].astype(F32)

    copies[0].wait()

    def cot_step(i, carry):
        pad_cot[pl.ds(pl.multiple_of(i * PITCH, 16) + 8, 128), :] = cot_rows(i)
        shifted_row(pad_cot, x3_cot, i)
        return carry

    lax.fori_loop(2, 34, cot_step, 0)

    def fill_edges(pad, which):
        for side, columns in enumerate(((0, 1), (126, 127))):
            for j, x in enumerate(columns):
                edge_send[which, side, j] = pad[
                    pl.ds(2 * PITCH + 8 + x, 32, stride=PITCH), :
                ].astype(BF)

    fill_edges(pad_cot, 0)
    cot_sides = column_halos(0)
    for copy in cot_sides:
        copy.start()
    cot_halos = cot_halos + cot_sides

    copies[2].wait()
    copies[3].wait()
    for wp in (wp_first, wp_second, wp_first_f, wp_second_f):
        wp[1152:1536, 0:128] = jnp.zeros((384, 128), BF)
        wp[0:384, 128:256] = jnp.zeros((384, 128), BF)
    for raw, wp, wp_f in ((first_v, wp_first, wp_first_f), (second_v, wp_second, wp_second_f)):
        for a in range(3):
            for e in range(3):
                tap = raw[a, e]
                turned = raw[2 - a, 2 - e].astype(F32).T.astype(BF)
                low = a * 384 + e * 128
                for target, value in ((wp, tap), (wp_f, turned)):
                    target[low : low + 128, 0:128] = value
                    target[low + 384 : low + 512, 128:256] = value

    inner = (tuple(range(2, 18, 2)), tuple(range(18, 32, 2)))

    def rows_of_pairs(pair, starts):
        for p, start in enumerate(starts):
            for k in range(2):
                yield start + k, pair[p * 128 : (p + 1) * 128, k * 128 : (k + 1) * 128]

    for starts in inner:
        for row, value in rows_of_pairs(pair_conv(x3_cot, wp_second_f, starts), starts):
            grad_act[rows_of(row), :] = value

    for slot in range(4):
        slot_copies[slot].wait()

        def turn(i, carry, slot=slot):
            piece = jnp.swapaxes(interp_v[slot, pl.ds(i * 32, 32)], 0, 1)
            where = pl.ds(pl.multiple_of(slot * 128 + i * 32, 32), 32)
            for y in range(32):
                weights_it[where, y * 128 : (y + 1) * 128] = piece[y]
            return carry

        lax.fori_loop(0, 4, turn, 0)

    copies[1].wait()
    copies[4].wait()
    copies[5].wait()
    for copy in coarse_copies:
        copy.wait()
    local_ids = [jnp.clip(ids[k] - (r - 1) * 8, 0, 23) for k in range(4)]
    picked = jnp.concatenate([window[local_ids[k]] for k in range(4)], 1)
    mix[...] = lax.dot_general(
        picked, lift_v[...], (((0,), (0,)), ((), ())), preferred_element_type=F32
    ).astype(BF)

    def stem_part(part):
        lifted = lax.dot_general(
            weights_it[:, part * 1024 : part * 1024 + 1024],
            mix[...],
            (((0,), (0,)), ((), ())),
            preferred_element_type=F32,
        ).reshape(8, 128, 128)
        stem = (fine_v[part * 8 : part * 8 + 8].astype(F32) + lifted).astype(BF)
        stem_v[part * 8 : part * 8 + 8] = stem
        for k in range(8):
            pad_stem[pl.ds((part * 8 + k + 2) * PITCH + 8, 128), :] = stem[k].astype(F32)

    stem_part(0)
    stem_part(3)
    stem_halos = row_halos(1, stem_v)
    for copy in stem_halos:
        copy.start()
    stem_part(1)
    stem_part(2)
    fill_edges(pad_stem, 1)
    stem_sides = column_halos(1)
    for copy in stem_sides:
        copy.start()
    stem_halos = stem_halos + stem_sides

    def stem_shift(row, carry):
        shifted_row(pad_stem, x3_stem, row)
        return carry

    lax.fori_loop(2, 34, stem_shift, 0, unroll=2)

    def put(row, act, pre):
        where = pl.ds((row + 1) * PITCH + 8, 128)
        pad_act[where, :] = act
        pad_pre[where, :] = pre

    for starts in inner:
        for row, value in rows_of_pairs(pair_conv(x3_stem, wp_first, starts), starts):
            put(row, *gate(value, grad_act[rows_of(row), :]))

    def keep(row, begin, size):
        where = pl.multiple_of(row * 128 + begin, 16)
        pre_z[row, begin : begin + size] = x3_pre[pl.ds(where, size), 128:256]

    def shift_step(row, carry):
        shifted_row(pad_act, x3_act, row)
        shifted_row(pad_pre, x3_pre, row)
        keep(row, 0, 128)
        return carry

    lax.fori_loop(3, 33, shift_step, 0, unroll=2)

    has_up = (r > 0).astype(F32)
    has_down = (r < n_row - 1).astype(F32)
    has_left = (c > 0).astype(F32)
    has_right = (c < n_col - 1).astype(F32)

    def take_halos(which, pad, x3):
        for side, (row, there) in enumerate(((0, has_up), (34, has_down))):
            for k in range(2):
                pad[pl.ds((row + k) * PITCH + 8, 128), :] = (
                    land_row[which, side, k].astype(F32) * there
                )
        for side, (column, there) in enumerate(((6, has_left), (136, has_right))):
            for j in range(2):
                pad[pl.ds(2 * PITCH + column + j, 32, stride=PITCH), :] = (
                    land_col[which, side, j].astype(F32) * there
                )
        for corner in range(4):
            low, side = divmod(corner, 2)
            there = (has_up, has_down)[low] * (has_left, has_right)[side]
            for j in range(2):
                tile = land_corner[which, corner, j].astype(F32) * there
                for k in range(2):
                    source = k if low else 14 + k
                    row = 34 + k if low else k
                    column = (6, 136)[side] + j
                    pad[pl.ds(row * PITCH + column, 1), :] = tile[source : source + 1]
        for row in (0, 1, 34, 35):
            shifted_row(pad, x3, row)

        def patch(row, carry):
            base = pl.multiple_of(row * 128, 128)
            start = row * PITCH + 8
            x3[pl.ds(base, 16), 0:128] = pad[pl.ds(start - 1, 16), :].astype(BF)
            x3[pl.ds(base + 112, 16), 256:384] = pad[pl.ds(start + 113, 16), :].astype(BF)
            return carry

        lax.fori_loop(2, 34, patch, 0)

    for copy in cot_halos:
        copy.wait()
    take_halos(0, pad_cot, x3_cot)
    outer = (0, 32)
    side_grad = side_conv(pad_cot, wp_second_f)
    for row, value in rows_of_pairs(pair_conv(x3_cot, wp_second_f, outer), outer):
        grad_act[rows_of(row), :] = value
    for copy in stem_halos:
        copy.wait()
    take_halos(1, pad_stem, x3_stem)
    for row, value in rows_of_pairs(pair_conv(x3_stem, wp_first, outer), outer):
        put(row, *gate(value, grad_act[rows_of(row), :]))
    side_act, side_pre = gate(side_conv(pad_stem, wp_first), side_grad)
    for side, (column, there) in enumerate(zip(SIDES, (has_left, 1.0, 1.0, has_right))):
        where = pl.ds(PITCH + column, 40, stride=PITCH)
        pad_act[where, :] = side_act[side * 40 : side * 40 + 40] * there
        pad_pre[where, :] = side_pre[side * 40 : side * 40 + 40] * there

    blank = jnp.zeros((PITCH, 128), F32)

    @pl.when(r == 0)
    def _():
        pad_act[pl.ds(PITCH, PITCH), :] = blank
        pad_pre[pl.ds(PITCH, PITCH), :] = blank

    @pl.when(r == n_row - 1)
    def _():
        pad_act[pl.ds(34 * PITCH, PITCH), :] = blank
        pad_pre[pl.ds(34 * PITCH, PITCH), :] = blank

    for row in (1, 2, 33, 34):
        shifted_row(pad_act, x3_act, row)
        shifted_row(pad_pre, x3_pre, row)
    keep(2, 0, 128)
    keep(33, 0, 128)

    def mend_step(row, carry):
        base = row * 128
        start = row * PITCH + 8
        for pad, x3 in ((pad_act, x3_act), (pad_pre, x3_pre)):
            for x in (0, 112):
                for e in range(3):
                    x3[pl.ds(pl.multiple_of(base + x, 16), 16), e * 128 : (e + 1) * 128] = pad[
                        pl.ds(start + x + e - 1, 16), :
                    ].astype(BF)
        keep(row, 0, 16)
        keep(row, 112, 16)
        return carry

    lax.fori_loop(3, 33, mend_step, 0, unroll=2)

    def tap_grad(x3, grad, group):
        total = None
        for begin, rows in ((1, 12), (13, 12), (25, 10)):
            lhs = x3[rows_of(begin, rows), :]
            rhs = jnp.concatenate(
                [
                    grad[pl.ds(begin + 1 - a, rows)].reshape(rows * 128, 128)
                    for a in range(3)
                ],
                1,
            )
            part = lax.dot_general(
                lhs, rhs, (((0,), (0,)), ((), ())), preferred_element_type=F32
            )
            if begin == 1:
                taps[...] = part
            else:
                taps[...] += part
        for a in range(3):
            local[group, a * 384 : (a + 1) * 384] = taps[:, a * 128 : (a + 1) * 128].astype(BF)


    def step0(group):
        rows = nq * SIZES[group] // 4
        return [
            pltpu.make_async_remote_copy(
                local.at[
                    group, pl.ds(pl.multiple_of((1 - h) * 4 * rows + k * rows, 16), rows)
                ],
                land0.at[group, k * rows : (k + 1) * rows],
                s0_send.at[group, k],
                s0_recv.at[group, k],
                (r, sibling),
                MESH,
            )
            for k in range(4)
        ]

    def step1(group):
        return [
            pltpu.make_async_remote_copy(
                half.at[group, peer, 0 : SIZES[group]],
                land1.at[group, q, 0 : SIZES[group]],
                s1_send.at[group, peer],
                s1_recv.at[group, q],
                (r, 2 * peer + h),
                MESH,
            )
            for peer in q_peers
        ]

    def step2(group):
        mine = land2.at[group, r] if group < 2 else land2.at[group, r, 48:64]
        sends = [
            pltpu.make_async_remote_copy(
                mine, mine, s2_send.at[group, peer], s2_recv.at[group, r], (peer, c), MESH
            )
            for peer in r_peers
        ]
        if group < 2:
            return sends
        blocks = [
            pltpu.make_async_remote_copy(
                land2.at[group, r, low : low + 16],
                land2.at[group, r, low : low + 16],
                blocks_send.at[k],
                blocks_recv.at[k],
                (to, c),
                MESH,
            )
            for k, (low, to) in enumerate(((0, up), (32, down)))
        ]
        return blocks + sends

    def chunk_of(group, owner):
        rows = CHUNK if group < 2 else 16
        return final.at[group, owner, 0:rows]

    def step3(group):
        mine = chunk_of(group, own)
        return [
            pltpu.make_async_remote_copy(
                mine,
                mine,
                s3_send.at[group, peer],
                s3_recv.at[group, q],
                (r, 2 * peer + h),
                MESH,
            )
            for peer in q_peers
        ]

    def step4(group, k):
        theirs = chunk_of(group, h * nq + k)
        return pltpu.make_async_remote_copy(
            theirs, theirs, s4_send.at[group, k], s4_recv.at[group, k], (r, sibling), MESH
        )

    def await_copy(landed, sem):
        pltpu.make_async_remote_copy(landed, landed, sem, sem, (r, sibling), MESH).wait_recv()

    def start_all(copies):
        for copy in copies:
            copy.start()

    def end_step0(group, copies):
        for copy in copies:
            copy.wait()
        size = SIZES[group]
        sends = step1(group)
        for k, peer in enumerate(q_peers + [q]):
            mine = local[
                group, pl.ds(pl.multiple_of((h * nq + peer) * size, 16), size)
            ].astype(F32)
            theirs = land0[group, pl.ds(pl.multiple_of(peer * size, 16), size)].astype(F32)
            half[group, peer, 0:size] = (mine + theirs).astype(BF)
            if k < nq - 1:
                sends[k].start()
        return sends

    def end_step1(group, sends):
        size = SIZES[group]
        for peer in q_peers:
            await_copy(land1.at[group, peer, 0:size], s1_recv.at[group, peer])
        land1[group, q, 0:size] = half[group, q, 0:size]
        total = land1[group, 0, 0:size].astype(F32)
        for k in range(1, nq):
            total = total + land1[group, k, 0:size].astype(F32)
        land2[group, r, 0:size] = total.astype(BF)
        following = step2(group)
        start_all(following)
        for copy in sends:
            copy.wait_send()
        return following

    def end_step2(group, sends):
        if group < 2:
            for peer in r_peers:
                await_copy(land2.at[group, peer], s2_recv.at[group, peer])
            total = land2[group, 0].astype(F32)
            for k in range(1, n_row):
                total = total + land2[group, k].astype(F32)
            final[group, own] = (total * (1.0 / 1024.0)).astype(BF)
        else:
            await_copy(land2.at[group, up, 32:48], blocks_recv.at[1])
            await_copy(land2.at[group, down, 0:16], blocks_recv.at[0])
            owned = (
                land2[group, r, 16:32].astype(F32)
                + land2[group, up, 32:48].astype(F32) * has_up
                + land2[group, down, 0:16].astype(F32) * has_down
            )
            final[group, own, 0:16] = owned.astype(BF)
        following = step3(group)
        start_all(following)
        for copy in sends:
            copy.wait_send()
        return following

    def lift_step2():
        for peer in r_peers:
            await_copy(land2.at[2, peer, 48:64], s2_recv.at[2, peer])
        total = land2[2, 0, 48:64].astype(F32)
        for k in range(1, n_row):
            total = total + land2[2, k, 48:64].astype(F32)
        lift_sum[h] = (total * (1.0 / 1024.0)).astype(BF)
        copy = pltpu.make_async_remote_copy(
            lift_sum.at[h], lift_sum.at[h], lift_send, lift_recv, (r, sibling), MESH
        )
        copy.start()
        return copy

    def end_step3(group, sends):
        passed = [step4(group, q)]
        passed[0].start()
        for peer in reversed(q_peers):
            landed = chunk_of(group, h * nq + peer)
            pltpu.make_async_remote_copy(
                landed, landed, s3_send.at[group, peer], s3_recv.at[group, peer],
                (r, sibling), MESH,
            ).wait_recv()
            copy = step4(group, peer)
            copy.start()
            passed.append(copy)
        for copy in sends:
            copy.wait_send()
        return passed

    def end_step4(group, passed):
        for copy in passed:
            copy.wait_send()
        for k in range(nq):
            landed = chunk_of(group, (1 - h) * nq + k)
            pltpu.make_async_remote_copy(
                landed, landed, s4_send.at[group, k], s4_recv.at[group, k], (r, sibling), MESH
            ).wait_recv()

    tap_grad(x3_act, cot_z, 0)
    pend_a = step0(0)
    start_all(pend_a)
    tap_grad(x3_stem, pre_z, 1)
    pend_a = end_step0(0, pend_a)
    pend_b = step0(1)
    start_all(pend_b)

    for part in range(2):
        starts = tuple(range(1 + 16 * part, 17 + 16 * part, 2))
        pair = pair_conv(x3_pre, wp_first_f, starts)
        for p in range(8):
            for k in range(2):
                row = 16 * part + 2 * p + k
                grad_fine[row] = (
                    pair[p * 128 : (p + 1) * 128, k * 128 : (k + 1) * 128] + cot_rows(row + 2)
                ).astype(BF)
    pend_b = end_step0(1, pend_b)

    moment = jnp.zeros((512, 128), F32)
    for part in range(4):
        moment = moment + jnp.dot(
            weights_it[:, part * 1024 : (part + 1) * 1024],
            grad_fine[part * 8 : part * 8 + 8].reshape(1024, 128),
            preferred_element_type=F32,
        )
    moment = moment.astype(BF)
    lift_part = jnp.dot(picked, moment, preferred_element_type=F32)
    blocks = lax.dot_general(
        lift_v[...], moment, (((1,), (1,)), ((), ())), preferred_element_type=F32
    )
    lift_part = lift_part.astype(BF)
    for section in range(3):
        for n in range(8):
            value = jnp.zeros((32, 128), F32)
            for k in range(4):
                value = value + jnp.where(
                    local_ids[k] == section * 8 + n, blocks[:, k * 128 : (k + 1) * 128], 0.0
                )
            value = value.astype(BF)
            for side in range(2):
                low = (2 * n + side) * SIZES[2] + section * 16
                local[2, low : low + 16] = value[side * 16 : side * 16 + 16]
    for owner in range(n_col):
        low = owner * SIZES[2] + 48
        part = owner // nq * 16
        local[2, low : low + 16] = lift_part[part : part + 16]
    pend_c = step0(2)
    start_all(pend_c)
    pend_a = end_step1(0, pend_a)

    def output_part(part):
        starts = tuple(range(1 + 16 * part, 17 + 16 * part, 2))
        for row, value in rows_of_pairs(pair_conv(x3_act, wp_second, starts), starts):
            out[row - 1] = (value + stem_v[row - 1].astype(F32)).astype(BF)

    output_part(0)
    pend_c = end_step0(2, pend_c)
    pend_b = end_step1(1, pend_b)
    output_part(1)
    pend_a = end_step2(0, pend_a)
    pend_c = end_step1(2, pend_c)
    pend_b = end_step2(1, pend_b)

    def widen(group, target):
        for a in range(3):
            for e in range(3):
                for part in range(8):
                    low = (a * 3 + e) * 128 + part * 16
                    owner, at = divmod(low, CHUNK)
                    target[a, e, part * 16 : part * 16 + 16] = final[
                        group, owner, at : at + 16
                    ].astype(F32)

    pend_c = end_step2(2, pend_c)
    pend_a = end_step3(0, pend_a)
    lift_copy = lift_step2()
    end_step4(0, pend_a)
    widen(0, grad_second)
    pend_b = end_step3(1, pend_b)
    pend_c = end_step3(2, pend_c)
    lift_copy.wait_send()
    await_copy(lift_sum.at[1 - h], lift_recv)
    for part in range(2):
        grad_lift[part * 16 : part * 16 + 16] = lift_sum[part].astype(F32)
    end_step4(1, pend_b)
    widen(1, grad_first)
    end_step4(2, pend_c)
    for n in range(8):
        for side in range(2):
            grad_coarse[n, side * 16 : side * 16 + 16] = final[2, 2 * n + side, 0:16].astype(F32)


def hand_over(*refs):
    sems = refs[12]
    copies = []
    for k in range(6):
        source, target = refs[k], refs[6 + k]
        pieces = 4 if k < 2 else 1
        size = source.shape[0] // pieces
        for p in range(pieces):
            part = pl.ds(p * size, size)
            copies.append(pltpu.make_async_copy(source.at[part], target.at[part], sems.at[k, p]))
    for copy in copies:
        copy.start()
    for copy in copies:
        copy.wait()


def body(n_row, n_col, fine, coarse, block_map, interp, lift, first, second, cot):
    anywhere = pl.BlockSpec(memory_space=pl.ANY)
    nq = n_col // 2
    dma = pltpu.SemaphoreType.DMA

    def vm(shape, dtype=BF):
        return pltpu.VMEM(shape, dtype)

    pad = vm((42 * PITCH, 128), F32)
    x3 = vm((36 * 128, 384))
    wp = vm((1536, 256))
    tile = vm((32, 128, 128))
    scratch = [
        tile,
        vm((4, 128, 32, 128)),
        vm((512, 4096)),
        vm((24, 32, 128)),
        vm((32, 128)),
        vm((3, 3, 128, 128)),
        vm((3, 3, 128, 128)),
        wp, wp, wp, wp,
        pad, pad, pad, pad,
        x3, x3, x3, x3,
        vm((36, 128, 128)),
        vm((36, 128, 128)),
        tile,
        vm((34 * 128, 128), F32),
        vm((512, 128)),
        vm((2, 2, 2, 32, 128)),
        vm((2, 2, 2, 128, 128)),
        vm((2, 2, 2, 32, 128)),
        vm((2, 4, 2, 16, 128)),
        vm((384, 384), F32),
        vm((3, n_col * CHUNK, 128)),
        vm((3, nq * CHUNK, 128)),
        vm((3, nq, CHUNK, 128)),
        vm((3, nq, CHUNK, 128)),
        vm((3, n_row, CHUNK, 128)),
        vm((3, n_col, CHUNK, 128)),
        dma((10,)),
        dma((2,)), dma((2,)),
        dma((2, 8)), dma((2, 8)),
        dma((3, 4)), dma((3, 4)),
        dma((3, nq)), dma((3, nq)),
        dma((3, n_row)), dma((3, n_row)),
        dma((3, nq)), dma((3, nq)),
        dma((3, nq)), dma((3, nq)),
        dma((2,)), dma((2,)), dma, dma,
        vm((2, 16, 128)),
    ]
    def handed(shape, dtype):
        return pltpu.VMEM(shape, dtype)

    shapes = (
        handed(fine.shape, BF),
        handed(fine.shape, BF),
        handed(coarse.shape, F32),
        handed(first.shape, F32),
        handed(second.shape, F32),
        handed(lift.shape, F32),
    )
    results = pl.pallas_call(
        functools.partial(kernel, n_row, n_col),
        out_shape=shapes,
        in_specs=[
            anywhere, anywhere, pl.BlockSpec(memory_space=pltpu.SMEM),
            anywhere, anywhere, anywhere, anywhere, anywhere,
        ],
        out_specs=tuple([pl.BlockSpec(memory_space=pltpu.VMEM)] * 6),
        scratch_shapes=scratch,
        compiler_params=pltpu.CompilerParams(
            collective_id=0, has_side_effects=True, vmem_limit_bytes=56 * 1024 * 1024
        ),
        name="step",
    )(fine, coarse, block_map.reshape(-1), interp, lift, first, second, cot)
    return pl.pallas_call(
        hand_over,
        out_shape=tuple(jax.ShapeDtypeStruct(x.shape, x.dtype) for x in results),
        in_specs=[pl.BlockSpec(memory_space=pltpu.VMEM)] * 6,
        out_specs=tuple([anywhere] * 6),
        scratch_shapes=[dma((6, 4))],
        name="hand_over",
        compiler_params=pltpu.CompilerParams(vmem_limit_bytes=1024 * 1024),
    )(*results)


def solution(mesh):
    n_row, n_col = mesh.shape["row"], mesh.shape["col"]
    return jax.shard_map(
        functools.partial(body, n_row, n_col),
        mesh=mesh,
        in_specs=(
            P("row", "col", None),
            P("row", None, None),
            P("row", "col", None),
            P(None, None, "row", "col"),
            P(),
            P(),
            P(),
            P("row", "col", None),
        ),
        out_specs=(
            P("row", "col", None),
            P("row", "col", None),
            P("row", None, None),
            P(),
            P(),
            P(),
        ),
        check_vma=False,
    )
```

```python
import functools

import jax
import jax.numpy as jnp
from jax import lax
from jax.experimental import pallas as pl
from jax.experimental.pallas import tpu as pltpu
from jax.sharding import PartitionSpec as P

MESH = pl.DeviceIdType.MESH
BF = jnp.bfloat16
F32 = jnp.float32
PITCH = 144
CHUNK = 80
SIZES = (CHUNK, CHUNK, 64)


def rows_of(row, count=1, pitch=128):
    start = row * pitch
    if not isinstance(start, int):
        start = pl.multiple_of(start, pitch if pitch == 128 else 16)
    return pl.ds(start, count * pitch)


def pair_conv(x3, wp, starts):
    parts = []
    for j in range(4):
        parts.append(jnp.concatenate([x3[rows_of(start + j), :] for start in starts], 0))
    return jnp.dot(jnp.concatenate(parts, 1), wp[...], preferred_element_type=F32)


SIDES = (7, 8, 135, 136)


def side_conv(pad, wp):
    sides = []
    for column in SIDES:
        sides.append(
            jnp.concatenate(
                [
                    pad[pl.ds(a * PITCH + column - 1 + e, 40, stride=PITCH), :].astype(BF)
                    for a in range(3)
                    for e in range(3)
                ],
                1,
            )
        )
    return jnp.dot(
        jnp.concatenate(sides, 0), wp[0:1152, 0:128], preferred_element_type=F32
    )


def shifted_row(pad, x3, row):
    start = row * PITCH + 8
    for e in range(3):
        x3[rows_of(row), e * 128 : (e + 1) * 128] = pad[pl.ds(start + e - 1, 128), :].astype(BF)


def gate(pre, grad):
    s = 0.5 * (1.0 + jnp.tanh(0.5 * pre))
    return pre * s, grad * (s * (1.0 + pre * (1.0 - s)))


def kernel(
    n_row,
    n_col,
    fine,
    coarse,
    ids,
    interp,
    lift,
    first,
    second,
    cot,
    out,
    grad_fine,
    grad_coarse,
    grad_first,
    grad_second,
    grad_lift,
    fine_v,
    interp_v,
    weights_it,
    window,
    lift_v,
    first_v,
    second_v,
    wp_first,
    wp_second,
    wp_first_f,
    wp_second_f,
    pad_cot,
    pad_stem,
    pad_act,
    pad_pre,
    x3_cot,
    x3_stem,
    x3_act,
    x3_pre,
    cot_z,
    pre_z,
    stem_v,
    grad_act,
    mix,
    edge_send,
    land_row,
    land_col,
    corner_send,
    land_corner,
    taps,
    local,
    land0,
    half,
    land1,
    land2,
    final,
    copy_sem,
    coarse_send,
    coarse_recv,
    halo_send,
    halo_recv,
    s0_send,
    s0_recv,
    s1_send,
    s1_recv,
    s2_send,
    s2_recv,
    s3_send,
    s3_recv,
    s4_send,
    s4_recv,
    blocks_send,
    blocks_recv,
    lift_send,
    lift_recv,
    lift_sum,
):
    r = lax.axis_index("row")
    c = lax.axis_index("col")
    nq = n_col // 2
    q = lax.div(c, 2)
    h = lax.rem(c, 2)
    sibling = c + 1 - 2 * h
    own = h * nq + q
    up = lax.rem(r + n_row - 1, n_row)
    down = lax.rem(r + 1, n_row)
    left = lax.rem(c + n_col - 1, n_col)
    right = lax.rem(c + 1, n_col)
    q_peers = [lax.rem(q + d, nq) for d in range(1, nq)]
    r_peers = [lax.rem(r + d, n_row) for d in range(1, n_row)]

    around = [
        (up, c), (down, c), (r, left), (r, right),
        (up, left), (up, right), (down, left), (down, right),
    ]
    barrier = pltpu.get_barrier_semaphore()
    peers = (
        around
        + [(r, 2 * peer + h) for peer in q_peers]
        + [(peer, c) for peer in r_peers[1:-1]]
    )
    for peer in peers:
        pl.semaphore_signal(barrier, inc=1, device_id=peer, device_id_type=MESH)

    copies = [
        pltpu.make_async_copy(cot, cot_z.at[2:34], copy_sem.at[0]),
        pltpu.make_async_copy(coarse, window.at[8:16], copy_sem.at[1]),
        pltpu.make_async_copy(first, first_v, copy_sem.at[2]),
        pltpu.make_async_copy(second, second_v, copy_sem.at[3]),
        pltpu.make_async_copy(lift, lift_v, copy_sem.at[4]),
        pltpu.make_async_copy(fine, fine_v, copy_sem.at[5]),
    ]
    slot_copies = [
        pltpu.make_async_copy(interp.at[k], interp_v.at[k], copy_sem.at[6 + k]) for k in range(4)
    ]
    for copy in copies[0:5] + slot_copies + copies[5:6]:
        copy.start()

    zero_row = jnp.zeros((2, 128, 128), BF)
    cot_z[0:2] = zero_row
    cot_z[34:36] = zero_row
    pre_z[0:2] = zero_row
    pre_z[34:36] = zero_row

    def halo_copy(which, k, src, dst, device):
        return pltpu.make_async_remote_copy(
            src, dst, halo_send.at[which, k], halo_recv.at[which, k], device, MESH
        )

    def row_halos(which, source):
        return [
            halo_copy(which, 0, source.at[0:2], land_row.at[which, 1], (up, c)),
            halo_copy(which, 1, source.at[30:32], land_row.at[which, 0], (down, c)),
        ]

    def column_halos(which):
        edges = edge_send.at[which]
        return [
            halo_copy(which, 2, edges.at[0], land_col.at[which, 1], (r, left)),
            halo_copy(which, 3, edges.at[1], land_col.at[which, 0], (r, right)),
            halo_copy(which, 4, corner_send.at[which, 0], land_corner.at[which, 3], (up, left)),
            halo_copy(which, 5, corner_send.at[which, 1], land_corner.at[which, 2], (up, right)),
            halo_copy(which, 6, corner_send.at[which, 2], land_corner.at[which, 1], (down, left)),
            halo_copy(which, 7, corner_send.at[which, 3], land_corner.at[which, 0], (down, right)),
        ]

    pl.semaphore_wait(barrier, len(peers))
    coarse_copies = [
        pltpu.make_async_remote_copy(
            coarse, window.at[16:24], coarse_send.at[0], coarse_recv.at[0], (up, c), MESH
        ),
        pltpu.make_async_remote_copy(
            coarse, window.at[0:8], coarse_send.at[1], coarse_recv.at[1], (down, c), MESH
        ),
    ]
    cot_halos = row_halos(0, cot)
    for copy in coarse_copies + cot_halos:
        copy.start()

    def cot_rows(row):
        return cot_z[row].astype(F32)

    copies[0].wait()

    def cot_step(i, carry):
        pad_cot[pl.ds(pl.multiple_of(i * PITCH, 16) + 8, 128), :] = cot_rows(i)
        shifted_row(pad_cot, x3_cot, i)
        return carry

    lax.fori_loop(2, 34, cot_step, 0)

    def fill_edges(pad, which):
        for side, columns in enumerate(((0, 1), (126, 127))):
            for j, x in enumerate(columns):
                edge_send[which, side, j] = pad[
                    pl.ds(2 * PITCH + 8 + x, 32, stride=PITCH), :
                ].astype(BF)

    def fill_corners(pad, which):
        for corner in range(4):
            low, side = divmod(corner, 2)
            cells = [
                pad[pl.ds(((32 if low else 2) + k) * PITCH + 8 + (126 if side else 0) + j, 1), :]
                for j in range(2)
                for k in range(2)
            ]
            cells.append(jnp.zeros((12, 128), F32))
            corner_send[which, corner] = jnp.concatenate(cells, 0).astype(BF)

    fill_edges(pad_cot, 0)
    fill_corners(pad_cot, 0)
    cot_sides = column_halos(0)
    for copy in cot_sides:
        copy.start()
    cot_halos = cot_halos + cot_sides

    copies[2].wait()
    copies[3].wait()
    for wp in (wp_first, wp_second, wp_first_f, wp_second_f):
        wp[1152:1536, 0:128] = jnp.zeros((384, 128), BF)
        wp[0:384, 128:256] = jnp.zeros((384, 128), BF)
    for raw, wp, wp_f in ((first_v, wp_first, wp_first_f), (second_v, wp_second, wp_second_f)):
        for a in range(3):
            for e in range(3):
                tap = raw[a, e]
                turned = raw[2 - a, 2 - e].astype(F32).T.astype(BF)
                low = a * 384 + e * 128
                for target, value in ((wp, tap), (wp_f, turned)):
                    target[low : low + 128, 0:128] = value
                    target[low + 384 : low + 512, 128:256] = value

    inner = (tuple(range(2, 18, 2)), tuple(range(18, 32, 2)))

    def rows_of_pairs(pair, starts):
        for p, start in enumerate(starts):
            for k in range(2):
                yield start + k, pair[p * 128 : (p + 1) * 128, k * 128 : (k + 1) * 128]

    for starts in inner:
        for row, value in rows_of_pairs(pair_conv(x3_cot, wp_second_f, starts), starts):
            grad_act[rows_of(row), :] = value

    for slot in range(4):
        slot_copies[slot].wait()

        def turn(i, carry, slot=slot):
            piece = jnp.swapaxes(interp_v[slot, pl.ds(i * 32, 32)], 0, 1)
            where = pl.ds(pl.multiple_of(slot * 128 + i * 32, 32), 32)
            for y in range(32):
                weights_it[where, y * 128 : (y + 1) * 128] = piece[y]
            return carry

        lax.fori_loop(0, 4, turn, 0)

    copies[1].wait()
    copies[4].wait()
    copies[5].wait()
    for copy in coarse_copies:
        copy.wait()
    local_ids = [jnp.clip(ids[k] - (r - 1) * 8, 0, 23) for k in range(4)]
    picked = jnp.concatenate([window[local_ids[k]] for k in range(4)], 1)
    mix[...] = lax.dot_general(
        picked, lift_v[...], (((0,), (0,)), ((), ())), preferred_element_type=F32
    ).astype(BF)

    def stem_part(part):
        lifted = lax.dot_general(
            weights_it[:, part * 1024 : part * 1024 + 1024],
            mix[...],
            (((0,), (0,)), ((), ())),
            preferred_element_type=F32,
        ).reshape(8, 128, 128)
        stem = (fine_v[part * 8 : part * 8 + 8].astype(F32) + lifted).astype(BF)
        stem_v[part * 8 : part * 8 + 8] = stem
        for k in range(8):
            pad_stem[pl.ds((part * 8 + k + 2) * PITCH + 8, 128), :] = stem[k].astype(F32)

    stem_part(0)
    stem_part(3)
    stem_halos = row_halos(1, stem_v)
    for copy in stem_halos:
        copy.start()
    stem_part(1)
    stem_part(2)
    fill_edges(pad_stem, 1)
    fill_corners(pad_stem, 1)
    stem_sides = column_halos(1)
    for copy in stem_sides:
        copy.start()
    stem_halos = stem_halos + stem_sides

    def stem_shift(row, carry):
        shifted_row(pad_stem, x3_stem, row)
        return carry

    lax.fori_loop(2, 34, stem_shift, 0, unroll=2)

    def put(row, act, pre):
        where = pl.ds((row + 1) * PITCH + 8, 128)
        pad_act[where, :] = act
        pad_pre[where, :] = pre

    for starts in inner:
        for row, value in rows_of_pairs(pair_conv(x3_stem, wp_first, starts), starts):
            put(row, *gate(value, grad_act[rows_of(row), :]))

    def keep(row, begin, size):
        where = pl.multiple_of(row * 128 + begin, 16)
        pre_z[row, begin : begin + size] = x3_pre[pl.ds(where, size), 128:256]

    def shift_step(row, carry):
        shifted_row(pad_act, x3_act, row)
        shifted_row(pad_pre, x3_pre, row)
        keep(row, 0, 128)
        return carry

    lax.fori_loop(3, 33, shift_step, 0, unroll=2)

    has_up = (r > 0).astype(F32)
    has_down = (r < n_row - 1).astype(F32)
    has_left = (c > 0).astype(F32)
    has_right = (c < n_col - 1).astype(F32)

    def take_halos(which, pad, x3):
        for side, (row, there) in enumerate(((0, has_up), (34, has_down))):
            for k in range(2):
                pad[pl.ds((row + k) * PITCH + 8, 128), :] = (
                    land_row[which, side, k].astype(F32) * there
                )
        for side, (column, there) in enumerate(((6, has_left), (136, has_right))):
            for j in range(2):
                pad[pl.ds(2 * PITCH + column + j, 32, stride=PITCH), :] = (
                    land_col[which, side, j].astype(F32) * there
                )
        for corner in range(4):
            low, side = divmod(corner, 2)
            there = (has_up, has_down)[low] * (has_left, has_right)[side]
            tile = land_corner[which, corner].astype(F32) * there
            for j in range(2):
                for k in range(2):
                    source = 2 * j + k
                    row = 34 + k if low else k
                    column = (6, 136)[side] + j
                    pad[pl.ds(row * PITCH + column, 1), :] = tile[source : source + 1]
        for row in (0, 1, 34, 35):
            shifted_row(pad, x3, row)

        def patch(row, carry):
            base = pl.multiple_of(row * 128, 128)
            start = row * PITCH + 8
            x3[pl.ds(base, 16), 0:128] = pad[pl.ds(start - 1, 16), :].astype(BF)
            x3[pl.ds(base + 112, 16), 256:384] = pad[pl.ds(start + 113, 16), :].astype(BF)
            return carry

        lax.fori_loop(2, 34, patch, 0)

    for copy in cot_halos:
        copy.wait()
    take_halos(0, pad_cot, x3_cot)
    outer = (0, 32)
    side_grad = side_conv(pad_cot, wp_second_f)
    for row, value in rows_of_pairs(pair_conv(x3_cot, wp_second_f, outer), outer):
        grad_act[rows_of(row), :] = value
    for copy in stem_halos:
        copy.wait()
    take_halos(1, pad_stem, x3_stem)
    for row, value in rows_of_pairs(pair_conv(x3_stem, wp_first, outer), outer):
        put(row, *gate(value, grad_act[rows_of(row), :]))
    side_act, side_pre = gate(side_conv(pad_stem, wp_first), side_grad)
    for side, (column, there) in enumerate(zip(SIDES, (has_left, 1.0, 1.0, has_right))):
        where = pl.ds(PITCH + column, 40, stride=PITCH)
        pad_act[where, :] = side_act[side * 40 : side * 40 + 40] * there
        pad_pre[where, :] = side_pre[side * 40 : side * 40 + 40] * there

    blank = jnp.zeros((PITCH, 128), F32)

    @pl.when(r == 0)
    def _():
        pad_act[pl.ds(PITCH, PITCH), :] = blank
        pad_pre[pl.ds(PITCH, PITCH), :] = blank

    @pl.when(r == n_row - 1)
    def _():
        pad_act[pl.ds(34 * PITCH, PITCH), :] = blank
        pad_pre[pl.ds(34 * PITCH, PITCH), :] = blank

    for row in (1, 2, 33, 34):
        shifted_row(pad_act, x3_act, row)
        shifted_row(pad_pre, x3_pre, row)
    keep(2, 0, 128)
    keep(33, 0, 128)

    def mend_step(row, carry):
        base = row * 128
        start = row * PITCH + 8
        for pad, x3 in ((pad_act, x3_act), (pad_pre, x3_pre)):
            for x in (0, 112):
                for e in range(3):
                    x3[pl.ds(pl.multiple_of(base + x, 16), 16), e * 128 : (e + 1) * 128] = pad[
                        pl.ds(start + x + e - 1, 16), :
                    ].astype(BF)
        keep(row, 0, 16)
        keep(row, 112, 16)
        return carry

    lax.fori_loop(3, 33, mend_step, 0, unroll=2)

    def tap_grad(x3, grad, group):
        total = None
        for begin, rows in ((1, 12), (13, 12), (25, 10)):
            lhs = x3[rows_of(begin, rows), :]
            rhs = jnp.concatenate(
                [
                    grad[pl.ds(begin + 1 - a, rows)].reshape(rows * 128, 128)
                    for a in range(3)
                ],
                1,
            )
            part = lax.dot_general(
                lhs, rhs, (((0,), (0,)), ((), ())), preferred_element_type=F32
            )
            if begin == 1:
                taps[...] = part
            else:
                taps[...] += part
        for a in range(3):
            local[group, a * 384 : (a + 1) * 384] = taps[:, a * 128 : (a + 1) * 128].astype(BF)


    def step0(group):
        rows = nq * SIZES[group] // 4
        return [
            pltpu.make_async_remote_copy(
                local.at[
                    group, pl.ds(pl.multiple_of((1 - h) * 4 * rows + k * rows, 16), rows)
                ],
                land0.at[group, k * rows : (k + 1) * rows],
                s0_send.at[group, k],
                s0_recv.at[group, k],
                (r, sibling),
                MESH,
            )
            for k in range(4)
        ]

    def step1(group):
        return [
            pltpu.make_async_remote_copy(
                half.at[group, peer, 0 : SIZES[group]],
                land1.at[group, q, 0 : SIZES[group]],
                s1_send.at[group, peer],
                s1_recv.at[group, q],
                (r, 2 * peer + h),
                MESH,
            )
            for peer in q_peers
        ]

    def step2(group):
        mine = land2.at[group, r] if group < 2 else land2.at[group, r, 48:64]
        sends = [
            pltpu.make_async_remote_copy(
                mine, mine, s2_send.at[group, peer], s2_recv.at[group, r], (peer, c), MESH
            )
            for peer in r_peers
        ]
        if group < 2:
            return sends
        blocks = [
            pltpu.make_async_remote_copy(
                land2.at[group, r, low : low + 16],
                land2.at[group, r, low : low + 16],
                blocks_send.at[k],
                blocks_recv.at[k],
                (to, c),
                MESH,
            )
            for k, (low, to) in enumerate(((0, up), (32, down)))
        ]
        return blocks + sends

    def chunk_of(group, owner):
        rows = CHUNK if group < 2 else 16
        return final.at[group, owner, 0:rows]

    def step3(group):
        mine = chunk_of(group, own)
        return [
            pltpu.make_async_remote_copy(
                mine,
                mine,
                s3_send.at[group, peer],
                s3_recv.at[group, q],
                (r, 2 * peer + h),
                MESH,
            )
            for peer in q_peers
        ]

    def quarters(group, core):
        if group == 2:
            return [final.at[2, pl.ds(core * nq, nq), 0:16]]
        size = nq // 4
        return [final.at[group, pl.ds(core * nq + k * size, size)] for k in range(4)]

    def step4(group):
        return [
            pltpu.make_async_remote_copy(
                piece, piece, s4_send.at[group, k], s4_recv.at[group, k], (r, sibling), MESH
            )
            for k, piece in enumerate(quarters(group, h))
        ]

    def await_copy(landed, sem):
        pltpu.make_async_remote_copy(landed, landed, sem, sem, (r, sibling), MESH).wait_recv()

    def start_all(copies):
        for copy in copies:
            copy.start()

    def end_step0(group, copies):
        for copy in copies:
            copy.wait()
        size = SIZES[group]
        sends = step1(group)
        for k, peer in enumerate(q_peers + [q]):
            mine = local[
                group, pl.ds(pl.multiple_of((h * nq + peer) * size, 16), size)
            ].astype(F32)
            theirs = land0[group, pl.ds(pl.multiple_of(peer * size, 16), size)].astype(F32)
            half[group, peer, 0:size] = (mine + theirs).astype(BF)
            if k < nq - 1:
                sends[k].start()
        return sends

    def end_step1(group, sends):
        size = SIZES[group]
        for peer in q_peers:
            await_copy(land1.at[group, peer, 0:size], s1_recv.at[group, peer])
        land1[group, q, 0:size] = half[group, q, 0:size]
        total = land1[group, 0, 0:size].astype(F32)
        for k in range(1, nq):
            total = total + land1[group, k, 0:size].astype(F32)
        land2[group, r, 0:size] = total.astype(BF)
        following = step2(group)
        start_all(following)
        for copy in sends:
            copy.wait_send()
        return following

    def end_step2(group, sends):
        if group < 2:
            for peer in r_peers:
                await_copy(land2.at[group, peer], s2_recv.at[group, peer])
            total = land2[group, 0].astype(F32)
            for k in range(1, n_row):
                total = total + land2[group, k].astype(F32)
            final[group, own] = (total * (1.0 / 1024.0)).astype(BF)
        else:
            await_copy(land2.at[group, up, 32:48], blocks_recv.at[1])
            await_copy(land2.at[group, down, 0:16], blocks_recv.at[0])
            owned = (
                land2[group, r, 16:32].astype(F32)
                + land2[group, up, 32:48].astype(F32) * has_up
                + land2[group, down, 0:16].astype(F32) * has_down
            )
            final[group, own, 0:16] = owned.astype(BF)
        following = step3(group)
        start_all(following)
        for copy in sends:
            copy.wait_send()
        return following

    def lift_step2():
        for peer in r_peers:
            await_copy(land2.at[2, peer, 48:64], s2_recv.at[2, peer])
        total = land2[2, 0, 48:64].astype(F32)
        for k in range(1, n_row):
            total = total + land2[2, k, 48:64].astype(F32)
        lift_sum[h] = (total * (1.0 / 1024.0)).astype(BF)
        copy = pltpu.make_async_remote_copy(
            lift_sum.at[h], lift_sum.at[h], lift_send, lift_recv, (r, sibling), MESH
        )
        copy.start()
        return copy

    def end_step3(group, sends):
        for peer in q_peers:
            await_copy(chunk_of(group, h * nq + peer), s3_recv.at[group, peer])
        passed = step4(group)
        start_all(passed)
        for copy in sends:
            copy.wait_send()
        return passed

    def end_step4(group, passed):
        for copy in passed:
            copy.wait_send()
        for k, piece in enumerate(quarters(group, 1 - h)):
            await_copy(piece, s4_recv.at[group, k])

    tap_grad(x3_act, cot_z, 0)
    pend_a = step0(0)
    start_all(pend_a)
    tap_grad(x3_stem, pre_z, 1)
    pend_a = end_step0(0, pend_a)
    pend_b = step0(1)
    start_all(pend_b)

    for part in range(2):
        starts = tuple(range(1 + 16 * part, 17 + 16 * part, 2))
        pair = pair_conv(x3_pre, wp_first_f, starts)
        for p in range(8):
            for k in range(2):
                row = 16 * part + 2 * p + k
                grad_fine[row] = (
                    pair[p * 128 : (p + 1) * 128, k * 128 : (k + 1) * 128] + cot_rows(row + 2)
                ).astype(BF)
    pend_b = end_step0(1, pend_b)

    moment = jnp.zeros((512, 128), F32)
    for part in range(4):
        moment = moment + jnp.dot(
            weights_it[:, part * 1024 : (part + 1) * 1024],
            grad_fine[part * 8 : part * 8 + 8].reshape(1024, 128),
            preferred_element_type=F32,
        )
    moment = moment.astype(BF)
    lift_part = jnp.dot(picked, moment, preferred_element_type=F32)
    blocks = lax.dot_general(
        lift_v[...], moment, (((1,), (1,)), ((), ())), preferred_element_type=F32
    )
    lift_part = lift_part.astype(BF)
    for section in range(3):
        for n in range(8):
            value = jnp.zeros((32, 128), F32)
            for k in range(4):
                value = value + jnp.where(
                    local_ids[k] == section * 8 + n, blocks[:, k * 128 : (k + 1) * 128], 0.0
                )
            value = value.astype(BF)
            for side in range(2):
                low = (2 * n + side) * SIZES[2] + section * 16
                local[2, low : low + 16] = value[side * 16 : side * 16 + 16]
    for owner in range(n_col):
        low = owner * SIZES[2] + 48
        part = owner // nq * 16
        local[2, low : low + 16] = lift_part[part : part + 16]
    pend_c = step0(2)
    start_all(pend_c)
    pend_a = end_step1(0, pend_a)

    def output_part(part):
        starts = tuple(range(1 + 16 * part, 17 + 16 * part, 2))
        for row, value in rows_of_pairs(pair_conv(x3_act, wp_second, starts), starts):
            out[row - 1] = (value + stem_v[row - 1].astype(F32)).astype(BF)

    output_part(0)
    pend_c = end_step0(2, pend_c)
    pend_b = end_step1(1, pend_b)
    output_part(1)
    pend_a = end_step2(0, pend_a)
    pend_c = end_step1(2, pend_c)
    pend_b = end_step2(1, pend_b)

    def widen(group, target):
        for a in range(3):
            for e in range(3):
                for part in range(8):
                    low = (a * 3 + e) * 128 + part * 16
                    owner, at = divmod(low, CHUNK)
                    target[a, e, part * 16 : part * 16 + 16] = final[
                        group, owner, at : at + 16
                    ].astype(F32)

    pend_c = end_step2(2, pend_c)
    pend_a = end_step3(0, pend_a)
    lift_copy = lift_step2()
    pend_b = end_step3(1, pend_b)
    pend_c = end_step3(2, pend_c)
    end_step4(0, pend_a)
    widen(0, grad_second)
    lift_copy.wait_send()
    await_copy(lift_sum.at[1 - h], lift_recv)
    for part in range(2):
        grad_lift[part * 16 : part * 16 + 16] = lift_sum[part].astype(F32)
    end_step4(1, pend_b)
    widen(1, grad_first)
    end_step4(2, pend_c)
    for n in range(8):
        for side in range(2):
            grad_coarse[n, side * 16 : side * 16 + 16] = final[2, 2 * n + side, 0:16].astype(F32)


def hand_over(*refs):
    sems = refs[12]
    copies = []
    for k in range(6):
        source, target = refs[k], refs[6 + k]
        pieces = (4, 4, 1, 3, 3, 1)[k]
        size = source.shape[0] // pieces
        for p in range(pieces):
            part = pl.ds(p * size, size)
            copies.append(pltpu.make_async_copy(source.at[part], target.at[part], sems.at[k, p]))
    for copy in copies:
        copy.start()
    for copy in copies:
        copy.wait()


def body(n_row, n_col, fine, coarse, block_map, interp, lift, first, second, cot):
    anywhere = pl.BlockSpec(memory_space=pl.ANY)
    nq = n_col // 2
    dma = pltpu.SemaphoreType.DMA

    def vm(shape, dtype=BF):
        return pltpu.VMEM(shape, dtype)

    pad = vm((42 * PITCH, 128), F32)
    x3 = vm((36 * 128, 384))
    wp = vm((1536, 256))
    tile = vm((32, 128, 128))
    scratch = [
        tile,
        vm((4, 128, 32, 128)),
        vm((512, 4096)),
        vm((24, 32, 128)),
        vm((32, 128)),
        vm((3, 3, 128, 128)),
        vm((3, 3, 128, 128)),
        wp, wp, wp, wp,
        pad, pad, pad, pad,
        x3, x3, x3, x3,
        vm((36, 128, 128)),
        vm((36, 128, 128)),
        tile,
        vm((34 * 128, 128), F32),
        vm((512, 128)),
        vm((2, 2, 2, 32, 128)),
        vm((2, 2, 2, 128, 128)),
        vm((2, 2, 2, 32, 128)),
        vm((2, 4, 16, 128)),
        vm((2, 4, 16, 128)),
        vm((384, 384), F32),
        vm((3, n_col * CHUNK, 128)),
        vm((3, nq * CHUNK, 128)),
        vm((3, nq, CHUNK, 128)),
        vm((3, nq, CHUNK, 128)),
        vm((3, n_row, CHUNK, 128)),
        vm((3, n_col, CHUNK, 128)),
        dma((10,)),
        dma((2,)), dma((2,)),
        dma((2, 8)), dma((2, 8)),
        dma((3, 4)), dma((3, 4)),
        dma((3, nq)), dma((3, nq)),
        dma((3, n_row)), dma((3, n_row)),
        dma((3, nq)), dma((3, nq)),
        dma((3, nq)), dma((3, nq)),
        dma((2,)), dma((2,)), dma, dma,
        vm((2, 16, 128)),
    ]
    def handed(shape, dtype):
        return pltpu.VMEM(shape, dtype)

    shapes = (
        handed(fine.shape, BF),
        handed(fine.shape, BF),
        handed(coarse.shape, F32),
        handed(first.shape, F32),
        handed(second.shape, F32),
        handed(lift.shape, F32),
    )
    results = pl.pallas_call(
        functools.partial(kernel, n_row, n_col),
        out_shape=shapes,
        in_specs=[
            anywhere, anywhere, pl.BlockSpec(memory_space=pltpu.SMEM),
            anywhere, anywhere, anywhere, anywhere, anywhere,
        ],
        out_specs=tuple([pl.BlockSpec(memory_space=pltpu.VMEM)] * 6),
        scratch_shapes=scratch,
        compiler_params=pltpu.CompilerParams(
            collective_id=0, has_side_effects=True, vmem_limit_bytes=56 * 1024 * 1024
        ),
        name="step",
    )(fine, coarse, block_map.reshape(-1), interp, lift, first, second, cot)
    return pl.pallas_call(
        hand_over,
        out_shape=tuple(jax.ShapeDtypeStruct(x.shape, x.dtype) for x in results),
        in_specs=[pl.BlockSpec(memory_space=pltpu.VMEM)] * 6,
        out_specs=tuple([anywhere] * 6),
        scratch_shapes=[dma((6, 4))],
        name="hand_over",
        compiler_params=pltpu.CompilerParams(vmem_limit_bytes=1024 * 1024),
    )(*results)


def solution(mesh):
    n_row, n_col = mesh.shape["row"], mesh.shape["col"]
    return jax.shard_map(
        functools.partial(body, n_row, n_col),
        mesh=mesh,
        in_specs=(
            P("row", "col", None),
            P("row", None, None),
            P("row", "col", None),
            P(None, None, "row", "col"),
            P(),
            P(),
            P(),
            P("row", "col", None),
        ),
        out_specs=(
            P("row", "col", None),
            P("row", "col", None),
            P("row", None, None),
            P(),
            P(),
            P(),
        ),
        check_vma=False,
    )
```
